256 devices in a mesh: pipe: 4 (over z_hi), dp: 64 (over z_lo, x, y, core).
Axes of the slice: x: 4, y: 4, z: 8 (z_hi: 4, z_lo: 2; z = z_hi * 2 + z_lo), core: 2. Of those that a mesh axis runs over, the one named last changes fastest.
Arguments:
- saved: bfloat16 [2, 4, 8192, 4096], P(None, 'pipe', 'dp'), may hold values from -16 to 16
- grad_out: bfloat16 [8192, 4096], P('dp'), may hold values from -6 to 6
- gain: float32 [2, 4, 4096], P(None, 'pipe'), may hold values from 0.5 to 1.5
- w_value: bfloat16 [4, 4096, 512], P('pipe', 'dp'), may hold values from -0.09375 to 0.09375
Outputs:
- grad_x: bfloat16 [2, 4, 8192, 4096], P(None, 'pipe', 'dp')
- grad_w: float32 [4, 4096, 512], P('pipe', 'dp')
The draws below stay inside these ranges and needn't reach their ends.
All inputs are finite; a program needn't handle non-finite values.
Results may differ from the reference program's by a relative error of at most 0.012.
Values may be sent and summed in bfloat16 or wider, within the bound.
No kernel may reach another device: no remote copies, remote signals or barrier semaphores. Data moves between devices by JAX's collectives and lax.ppermute only.
A program may use at most 64 MiB of HBM per device.

```python
import jax
import jax.numpy as jnp
from jax import lax

HEAD = 128
Q_HEADS = 32
KV_HEADS = 4
D = 4096
KV = 512
TOKENS = 8192
N_PIPE = 4


def spiked(entries, own_key, source, target, blocks, factor):
    owner, partner = [(jnp.arange(entries.shape[position]) // (entries.shape[position] // blocks)).reshape([-1 if axis == position else 1 for axis in range(entries.ndim)]) for position in (source, target)]
    chosen = jax.random.permutation(own_key, blocks)[partner]
    strong = (owner == chosen) | (owner == (partner + blocks // 2) % blocks)
    return jnp.where(strong, factor * entries, entries)


def block_scale(stream_key, extent, split, low, top_value):
    loudness = 1.0
    for position, shards_of in split:
        draws = jax.random.uniform(jax.random.fold_in(jax.random.fold_in(stream_key, 6), position), (shards_of,), jnp.float32, low / len(split), top_value / len(split))
        loudness = loudness * jnp.repeat(jnp.exp(draws), extent[position] // shards_of).reshape((-1,) + (1,) * (len(extent) - 1 - position))
    return loudness


def gaussian(key, dims, deviation, reach, shards=(), dtype=jnp.bfloat16):
    entries = deviation * jax.random.normal(key, dims, jnp.float32)
    if shards:
        entries = entries * block_scale(key, dims, shards, -0.22, 0.18)
    return jnp.clip(entries, -reach, reach).astype(dtype)


def noise_with(rng, shape, deviation, reach, pieces, heavy, kind=jnp.bfloat16):
    values = deviation * jax.random.normal(rng, shape, jnp.float32)
    if pieces:
        values = values * block_scale(rng, shape, pieces, -0.22, 0.18)
    return jnp.clip(spiked(values, jax.random.fold_in(rng, 3), *heavy), -reach, reach).astype(kind)


def setup_inputs(seed: int = 0) -> dict:
    arg_keys = jax.random.split(jax.random.key(seed), 5)
    saved = noise_with(arg_keys[0], (2, N_PIPE, TOKENS, D), 1.0, 16.0, ((1, 4), (2, 64)), (2, 3, 64, 4.0))
    grad_out = gaussian(arg_keys[1], (TOKENS, D), 1.0, 6.0, ((0, 64),))
    gain = jnp.clip(1.0 + 0.1 * jax.random.normal(arg_keys[2], (2, N_PIPE, D), jnp.float32), 0.5, 1.5)
    w_value = gaussian(arg_keys[3], (N_PIPE, D, KV), D ** -0.5, 0.09375, ((0, 4), (1, 64)))
    return {"saved": saved, "grad_out": grad_out, "gain": gain, "w_value": w_value}


def section_back(x, dy, g, w_mat):
    x32 = x.astype(jnp.float32)
    rinv = lax.rsqrt(lax.optimization_barrier(jnp.mean(x32 * x32, axis=-1, keepdims=True)) + 1e-05)
    normed = x32 * rinv
    hidden = (normed * g).astype(jnp.bfloat16)
    rows = x.shape[0]
    dv = dy.astype(jnp.float32).reshape(rows, KV_HEADS, Q_HEADS // KV_HEADS, HEAD).sum(2)
    dv = dv.reshape(rows, KV_HEADS * HEAD).astype(jnp.bfloat16)
    dh = lax.dot_general(dv, w_mat, (((1,), (1,)), ((), ())), preferred_element_type=jnp.float32)
    dhg = dh * g
    dx = dy.astype(jnp.float32) + rinv * (dhg - normed * lax.optimization_barrier(jnp.mean(dhg * normed, axis=-1, keepdims=True)))
    dx = dx.astype(jnp.bfloat16)
    gw = lax.dot_general(hidden, dv, (((0,), (0,)), ((), ())), preferred_element_type=jnp.float32)
    return (dx, gw)

def reference(saved, grad_out, gain, w_value):
    dy = grad_out
    grads_x = {}
    grads_w = {}
    for section in range(2 * N_PIPE - 1, -1, -1):
        loop_id = section // N_PIPE
        pair = section % N_PIPE
        dx, gw = section_back(saved[loop_id, pair], dy, gain[loop_id, pair], w_value[pair])
        grads_x[loop_id, pair] = dx
        grads_w[pair] = gw if loop_id == 1 else grads_w[pair] + gw
        dy = dx
    grad_x = jnp.stack([jnp.stack([grads_x[l, p] for p in range(N_PIPE)]) for l in range(2)])
    grad_w = jnp.stack([grads_w[p] for p in range(N_PIPE)])
    return (grad_x, grad_w)
```

```python
import functools

import jax
import jax.numpy as jnp
from jax import lax
from jax.experimental import pallas as pl
from jax.experimental.pallas import tpu as pltpu
from jax.sharding import Mesh
from jax.sharding import PartitionSpec as P

HEAD = 128
ROWS = 16
SLACK = 2
DP = ("dp_0", "dp_1", "dp_2", "dp_3")
IN_VMEM = pl.BlockSpec(memory_space=pltpu.VMEM)
IN_SMEM = pl.BlockSpec(memory_space=pltpu.SMEM)
ANYWHERE = pl.BlockSpec(memory_space=pl.ANY)


def copy_for_each(array, axis):
    count = lax.axis_size(axis)
    return lax.all_to_all(
        jnp.broadcast_to(array[None], (count, *array.shape)), axis, 0, 0, tiled=True
    )


def gathered_rows(array):
    first = copy_for_each(array, DP[:3])
    tiles = jnp.swapaxes(copy_for_each(first, DP[3]), 0, 1)
    return tiles.reshape(-1, array.shape[-1])


def task_of(step, section, npipe):
    return step - SLACK * (npipe - 1 - section)


def step_kernel(step, npipe, blocks, where, w_ref, x_ref, g_ref, fresh_ref, in_ref, dx_ref, dv_ref):
    section = where[0]
    task = task_of(step, section, npipe)

    @pl.when((task >= 0) & (task < 2 * blocks))
    def _():
        later = task < blocks
        loop = jnp.where(later, 1, 0)
        block = jnp.where(later, task, task - blocks)
        row = pl.multiple_of(block * ROWS, ROWS)
        width = dx_ref.shape[1]
        kv_width = dv_ref.shape[1]
        heads = kv_width // HEAD
        group = width // kv_width
        take = later & (section == npipe - 1)
        dy = jnp.where(take, fresh_ref[pl.ds(row, ROWS), :], in_ref[...]).astype(jnp.float32)
        x = x_ref[loop, pl.ds(row, ROWS), :].astype(jnp.float32)
        sums = []
        for head in range(heads):
            base = head * group * HEAD
            total = dy[:, base : base + HEAD]
            for member in range(1, group):
                at = base + member * HEAD
                total = total + dy[:, at : at + HEAD]
            sums.append(total)
        dv = jnp.concatenate(sums, axis=1).astype(jnp.bfloat16)
        dv_ref[...] = dv
        dh = lax.dot_general(
            dv, w_ref[...], (((1,), (1,)), ((), ())), preferred_element_type=jnp.float32
        )
        dhg = dh * g_ref[loop]
        rinv = lax.rsqrt(jnp.mean(x * x, axis=-1, keepdims=True) + 1e-05)
        normed = x * rinv
        along = jnp.mean(dhg * normed, axis=-1, keepdims=True)
        dx_ref[...] = (dy + rinv * (dhg - normed * along)).astype(jnp.bfloat16)


def one_step(step, npipe, blocks, where, w_mat, x, gain, fresh, incoming):
    rows, width = incoming.shape
    kv_width = w_mat.shape[1]
    return pl.pallas_call(
        functools.partial(step_kernel, step, npipe, blocks),
        out_shape=(
            jax.ShapeDtypeStruct((rows, width), jnp.bfloat16),
            jax.ShapeDtypeStruct((rows, kv_width), jnp.bfloat16),
        ),
        in_specs=[IN_SMEM] + [IN_VMEM] * 5,
        out_specs=(IN_VMEM, IN_VMEM),
        compiler_params=pltpu.CompilerParams(vmem_limit_bytes=32 * 2**20),
        name="section_step",
    )(where, w_mat, x, gain, fresh, incoming)


def collect_kernel(npipe, blocks, where, *refs):
    *pieces, out_ref, sems = refs
    section = where[0]

    def each(act):
        for step, piece in enumerate(pieces):
            task = task_of(step, section, npipe)

            @pl.when((task >= 0) & (task < 2 * blocks))
            def _():
                later = task < blocks
                loop = jnp.where(later, 1, 0)
                row = pl.multiple_of((task - jnp.where(later, 0, blocks)) * ROWS, ROWS)
                target = out_ref.at[loop, pl.ds(row, ROWS), :]
                act(pltpu.make_async_copy(piece, target, sems.at[step]))

    each(lambda copy: copy.start())
    each(lambda copy: copy.wait())


def collected(where, pieces, npipe, blocks):
    width = pieces[0].shape[1]
    return pl.pallas_call(
        functools.partial(collect_kernel, npipe, blocks),
        out_shape=jax.ShapeDtypeStruct((2, blocks * ROWS, width), jnp.bfloat16),
        in_specs=[IN_SMEM] + [ANYWHERE] * len(pieces),
        out_specs=ANYWHERE,
        scratch_shapes=[pltpu.SemaphoreType.DMA((len(pieces),))],
        name="collect_rows",
    )(where, *pieces)


def on_device(saved, grad_out, gain, w_value):
    npipe = lax.axis_size("pipe")
    section = lax.axis_index("pipe")
    where = section.astype(jnp.int32).reshape(1)
    x = saved[:, 0]
    scale = gain
    _, tok, width = x.shape
    blocks = tok // ROWS
    w_mat = gathered_rows(w_value[0])
    kv_width = w_mat.shape[1]

    x32 = x.astype(jnp.float32)
    rinv = lax.rsqrt(jnp.mean(x32 * x32, axis=-1, keepdims=True) + 1e-05)
    hidden = (x32 * rinv * scale).astype(jnp.bfloat16)
    far, across = lax.axis_size("dp_0"), lax.axis_size("dp_1")
    near = width // (far * across)
    tiles = hidden.reshape(2, tok, far, across, near).transpose(3, 0, 1, 2, 4)
    tiles = tiles.reshape(across, 2, tok, far * near)
    tiles = lax.all_to_all(tiles, "dp_1", 0, 0, tiled=True)

    steps = 2 * blocks + SLACK * (npipe - 1)
    sent, gx_parts, gv_parts = {}, [], []
    for step in range(steps):
        incoming = sent.pop(step - SLACK, None)
        if incoming is None:
            incoming = jnp.zeros((ROWS, width), jnp.bfloat16)
        dx, dv = one_step(step, npipe, blocks, where, w_mat, x, scale, grad_out, incoming)
        gx_parts.append(dx)
        gv_parts.append(dv)
        pairs = []
        for source in range(npipe):
            task = task_of(step, source, npipe)
            if 0 <= task < (blocks if source == 0 else 2 * blocks):
                pairs.append((source, (source - 1) % npipe))
        if pairs:
            sent[step] = lax.ppermute(dx, "pipe", pairs)

    grad_x = collected(where, gx_parts, npipe, blocks)[:, None]

    offset = SLACK * (npipe - 1 - section) * ROWS
    span = blocks + SLACK * (npipe - 1)
    grad_w = None
    for loop, first in ((1, 0), (0, blocks)):
        stacked = jnp.concatenate(gv_parts[first : first + span], axis=0)
        dv = lax.dynamic_slice_in_dim(stacked, offset, tok, 0)
        everyone = copy_for_each(dv, "dp_1").reshape(across * tok, kv_width)
        rows = tiles[:, loop].reshape(across * tok, far * near)
        part = lax.dot_general(
            rows, everyone, (((0,), (0,)), ((), ())), preferred_element_type=jnp.float32
        )
        grad_w = part if grad_w is None else grad_w + part
    others = ("dp_0", "dp_2", "dp_3")
    count = lax.axis_size(others)
    pieces = grad_w.astype(jnp.bfloat16).reshape(count, -1, kv_width)
    arrived = lax.all_to_all(pieces, others, 0, 0, tiled=True)
    grad_w = arrived.astype(jnp.float32).sum(axis=0)[None]
    return (grad_x, grad_w)


def solution(mesh):
    finer = Mesh(
        mesh.devices.reshape(mesh.shape["pipe"], 2, 4, 4, 2),
        ("pipe", "dp_0", "dp_1", "dp_2", "dp_3"),
    )
    placed = (P(None, "pipe", DP, None), P(DP, None), P(None, "pipe", None), P("pipe", DP, None))
    return jax.shard_map(
        on_device,
        mesh=finer,
        in_specs=placed,
        out_specs=(P(None, "pipe", DP, None), P("pipe", DP, None)),
        check_vma=False,
    )
```

```python
import functools

import jax
import jax.numpy as jnp
from jax import lax
from jax.experimental import pallas as pl
from jax.experimental.pallas import tpu as pltpu
from jax.sharding import Mesh
from jax.sharding import PartitionSpec as P

HEAD = 128
ROWS = 16
SLACK = 2
DP = ("dp_0", "dp_1", "dp_2", "dp_3")
IN_VMEM = pl.BlockSpec(memory_space=pltpu.VMEM)
IN_SMEM = pl.BlockSpec(memory_space=pltpu.SMEM)
ANYWHERE = pl.BlockSpec(memory_space=pl.ANY)


def copy_for_each(array, axis):
    count = lax.axis_size(axis)
    return lax.all_to_all(
        jnp.broadcast_to(array[None], (count, *array.shape)), axis, 0, 0, tiled=True
    )


def gathered_rows(array):
    first = copy_for_each(array, DP[:3])
    tiles = jnp.swapaxes(copy_for_each(first, DP[3]), 0, 1)
    return tiles.reshape(-1, array.shape[-1])


def held_until(value, token):
    return pl.pallas_call(
        lambda value_ref, token_ref, out_ref: None,
        out_shape=jax.ShapeDtypeStruct(value.shape, value.dtype),
        in_specs=[ANYWHERE, ANYWHERE],
        out_specs=ANYWHERE,
        input_output_aliases={0: 0},
        name="held_until",
    )(value, token)


def task_of(step, section, npipe):
    return step - SLACK * (npipe - 1 - section)


def step_kernel(step, npipe, blocks, where, w_ref, x_ref, g_ref, fresh_ref, in_ref, dx_ref, dv_ref):
    section = where[0]
    task = task_of(step, section, npipe)

    @pl.when((task >= 0) & (task < 2 * blocks))
    def _():
        later = task < blocks
        loop = jnp.where(later, 1, 0)
        block = jnp.where(later, task, task - blocks)
        row = pl.multiple_of(block * ROWS, ROWS)
        width = dx_ref.shape[1]
        kv_width = dv_ref.shape[1]
        heads = kv_width // HEAD
        group = width // kv_width
        take = later & (section == npipe - 1)
        dy = jnp.where(take, fresh_ref[pl.ds(row, ROWS), :], in_ref[...]).astype(jnp.float32)
        x = x_ref[loop, pl.ds(row, ROWS), :].astype(jnp.float32)
        sums = []
        for head in range(heads):
            base = head * group * HEAD
            total = dy[:, base : base + HEAD]
            for member in range(1, group):
                at = base + member * HEAD
                total = total + dy[:, at : at + HEAD]
            sums.append(total)
        dv = jnp.concatenate(sums, axis=1).astype(jnp.bfloat16)
        dv_ref[...] = dv
        dh = lax.dot_general(
            dv, w_ref[...], (((1,), (1,)), ((), ())), preferred_element_type=jnp.float32
        )
        dhg = dh * g_ref[loop]
        rinv = lax.rsqrt(jnp.mean(x * x, axis=-1, keepdims=True) + 1e-05)
        normed = x * rinv
        along = jnp.mean(dhg * normed, axis=-1, keepdims=True)
        dx_ref[...] = (dy + rinv * (dhg - normed * along)).astype(jnp.bfloat16)


def one_step(step, npipe, blocks, where, w_mat, x, gain, fresh, incoming):
    rows, width = incoming.shape
    kv_width = w_mat.shape[1]
    return pl.pallas_call(
        functools.partial(step_kernel, step, npipe, blocks),
        out_shape=(
            jax.ShapeDtypeStruct((rows, width), jnp.bfloat16),
            jax.ShapeDtypeStruct((rows, kv_width), jnp.bfloat16),
        ),
        in_specs=[IN_SMEM] + [IN_VMEM] * 5,
        out_specs=(IN_VMEM, IN_VMEM),
        compiler_params=pltpu.CompilerParams(vmem_limit_bytes=32 * 2**20),
        name="section_step",
    )(where, w_mat, x, gain, fresh, incoming)


def collect_kernel(npipe, blocks, where, *refs):
    *pieces, out_ref, sems = refs
    section = where[0]

    def each(act):
        for step, piece in enumerate(pieces):
            task = task_of(step, section, npipe)

            @pl.when((task >= 0) & (task < 2 * blocks))
            def _():
                later = task < blocks
                loop = jnp.where(later, 1, 0)
                row = pl.multiple_of((task - jnp.where(later, 0, blocks)) * ROWS, ROWS)
                target = out_ref.at[loop, pl.ds(row, ROWS), :]
                act(pltpu.make_async_copy(piece, target, sems.at[step]))

    each(lambda copy: copy.start())
    each(lambda copy: copy.wait())


def collected(where, pieces, npipe, blocks):
    width = pieces[0].shape[1]
    return pl.pallas_call(
        functools.partial(collect_kernel, npipe, blocks),
        out_shape=jax.ShapeDtypeStruct((2, blocks * ROWS, width), jnp.bfloat16),
        in_specs=[IN_SMEM] + [IN_VMEM] * len(pieces),
        out_specs=ANYWHERE,
        scratch_shapes=[pltpu.SemaphoreType.DMA((len(pieces),))],
        name="collect_rows",
    )(where, *pieces)


def on_device(saved, grad_out, gain, w_value):
    npipe = lax.axis_size("pipe")
    section = lax.axis_index("pipe")
    where = section.astype(jnp.int32).reshape(1)
    x = saved[:, 0]
    scale = gain
    _, tok, width = x.shape
    blocks = tok // ROWS
    w_mat = gathered_rows(w_value[0])
    kv_width = w_mat.shape[1]

    x32 = x.astype(jnp.float32)
    rinv = lax.rsqrt(jnp.mean(x32 * x32, axis=-1, keepdims=True) + 1e-05)
    hidden = (x32 * rinv * scale).astype(jnp.bfloat16)
    far, across = lax.axis_size("dp_0"), lax.axis_size("dp_1")
    near = width // (far * across)
    tiles = hidden.reshape(2, tok, far, across, near).transpose(3, 0, 1, 2, 4)
    tiles = tiles.reshape(across, 2, tok, far * near)

    steps = 2 * blocks + SLACK * (npipe - 1)
    sent, gx_parts, gv_parts = {}, [], []
    for step in range(steps):
        incoming = sent.pop(step - SLACK, None)
        if incoming is None:
            incoming = jnp.zeros((ROWS, width), jnp.bfloat16)
        dx, dv = one_step(step, npipe, blocks, where, w_mat, x, scale, grad_out, incoming)
        gx_parts.append(dx)
        gv_parts.append(dv)
        if step == SLACK:
            tiles = lax.all_to_all(held_until(tiles, dv), "dp_1", 0, 0, tiled=True)
        pairs = []
        for source in range(npipe):
            task = task_of(step, source, npipe)
            if 0 <= task < (blocks if source == 0 else 2 * blocks):
                pairs.append((source, (source - 1) % npipe))
        if pairs:
            sent[step] = lax.ppermute(dx, "pipe", pairs)

    grad_x = collected(where, gx_parts, npipe, blocks)[:, None]

    offset = SLACK * (npipe - 1 - section) * ROWS
    span = blocks + SLACK * (npipe - 1)
    grad_w = None
    for loop, first in ((1, 0), (0, blocks)):
        stacked = jnp.concatenate(gv_parts[first : first + span], axis=0)
        dv = lax.dynamic_slice_in_dim(stacked, offset, tok, 0)
        everyone = copy_for_each(dv, "dp_1").reshape(across * tok, kv_width)
        rows = tiles[:, loop].reshape(across * tok, far * near)
        part = lax.dot_general(
            rows, everyone, (((0,), (0,)), ((), ())), preferred_element_type=jnp.float32
        )
        grad_w = part if grad_w is None else grad_w + part
    others = ("dp_0", "dp_2", "dp_3")
    count = lax.axis_size(others)
    pieces = grad_w.astype(jnp.bfloat16).reshape(count, -1, kv_width)
    arrived = lax.all_to_all(pieces, others, 0, 0, tiled=True)
    grad_w = arrived.astype(jnp.float32).sum(axis=0)[None]
    return (grad_x, grad_w)


def solution(mesh):
    finer = Mesh(
        mesh.devices.reshape(mesh.shape["pipe"], 2, 4, 4, 2),
        ("pipe", "dp_0", "dp_1", "dp_2", "dp_3"),
    )
    placed = (P(None, "pipe", DP, None), P(DP, None), P(None, "pipe", None), P("pipe", DP, None))
    return jax.shard_map(
        on_device,
        mesh=finer,
        in_specs=placed,
        out_specs=(P(None, "pipe", DP, None), P("pipe", DP, None)),
        check_vma=False,
    )
```

```python
import functools

import jax
import jax.numpy as jnp
from jax import lax
from jax.experimental import pallas as pl
from jax.experimental.pallas import tpu as pltpu
from jax.sharding import Mesh
from jax.sharding import PartitionSpec as P

HEAD = 128
CHUNK = 16
DP = ("dp_0", "dp_1", "dp_2", "dp_3")
IN_VMEM = pl.BlockSpec(memory_space=pltpu.VMEM)
IN_SMEM = pl.BlockSpec(memory_space=pltpu.SMEM)
ANYWHERE = pl.BlockSpec(memory_space=pl.ANY)
BF16, F32 = jnp.bfloat16, jnp.float32


def copy_for_each(array, axis):
    count = lax.axis_size(axis)
    return lax.all_to_all(
        jnp.broadcast_to(array[None], (count, *array.shape)), axis, 0, 0, tiled=True
    )


def kernel_call(kernel, name, out_shape, specs, operands, scratch=(), out_spec=IN_VMEM, room=8):
    return pl.pallas_call(
        kernel,
        out_shape=out_shape,
        in_specs=specs,
        out_specs=jax.tree.map(lambda _: out_spec, out_shape),
        scratch_shapes=list(scratch),
        compiler_params=pltpu.CompilerParams(vmem_limit_bytes=room * 2**20),
        name=name,
    )(*operands)


def held_until(value, token):
    return pl.pallas_call(
        lambda value_ref, token_ref, out_ref: None,
        out_shape=jax.ShapeDtypeStruct(value.shape, value.dtype),
        in_specs=[ANYWHERE, IN_VMEM],
        out_specs=ANYWHERE,
        input_output_aliases={0: 0},
        compiler_params=pltpu.CompilerParams(vmem_limit_bytes=2**20),
        name="held_until",
    )(value, token)


def folded(values, kv_width):
    group = values.shape[1] // kv_width
    sums = []
    for head in range(kv_width // HEAD):
        base = head * group * HEAD
        total = values[:, base : base + HEAD]
        for member in range(1, group):
            at = base + member * HEAD
            total = total + values[:, at : at + HEAD]
        sums.append(total)
    return jnp.concatenate(sums, axis=1)


def norm_kernel(where, x_ref, g_ref, fresh_ref, tiles_ref, q_ref, rinv_ref, dv_ref):
    _, tok, width = x_ref.shape
    kv_width = dv_ref.shape[1]
    across, _, _, part = tiles_ref.shape
    far = 2
    near = part // far

    def one(index, carry):
        row = pl.multiple_of(index * CHUNK, CHUNK)
        rows = pl.ds(row, CHUNK)
        dv_ref[rows, :] = folded(fresh_ref[rows, :].astype(F32), kv_width).astype(BF16)
        for loop in range(2):
            x = x_ref[loop, rows, :].astype(F32)
            rinv = lax.rsqrt(jnp.mean(x * x, axis=-1, keepdims=True) + 1e-05)
            normed = x * rinv
            rinv_ref[loop, rows, :] = jnp.broadcast_to(rinv, (CHUNK, HEAD))
            q_ref[loop, rows, :] = folded(normed, kv_width)
            hidden = (normed * g_ref[loop]).astype(BF16)
            for place in range(across):
                for half in range(far):
                    at = (half * across + place) * near
                    tiles_ref[lax.rem(place + across - where[1], across), loop, rows, half * near : (half + 1) * near] = hidden[
                        :, at : at + near
                    ]
        return carry

    lax.fori_loop(0, tok // CHUNK, one, 0)


def fold_kernel(where, mine_ref, other_ref, gcol_ref, tiles_ref, w_ref, f_ref, z_ref):
    width, kv_width = w_ref.shape
    count, piece, _ = mine_ref.shape
    for index in range(count):
        for ref, core in ((mine_ref, where[2]), (other_ref, 1 - where[2])):
            at = pl.multiple_of((2 * index + core) * piece, piece)
            w_ref[pl.ds(at, piece), :] = ref[index]
    across, _, tok, part = tiles_ref.shape
    far = 2
    near = part // far
    group = width // kv_width
    for head in range(kv_width // HEAD):
        for row in range(0, HEAD, CHUNK):
            totals = [None, None]
            for member in range(group):
                at = (head * group + member) * HEAD + row
                rows = w_ref[at : at + CHUNK, :].astype(F32)
                for loop in range(2):
                    term = rows * gcol_ref[at : at + CHUNK, loop : loop + 1]
                    totals[loop] = term if member == 0 else totals[loop] + term
            for loop in range(2):
                f_ref[loop, head * HEAD + row : head * HEAD + row + CHUNK, :] = totals[loop].astype(BF16)
    for loop in range(2):
        total = None
        for place in range(across):
            for half in range(far):
                at = (half * across + place) * near
                term = jnp.dot(
                    tiles_ref[
                        lax.rem(place + across - where[1], across),
                        loop,
                        :,
                        half * near : (half + 1) * near,
                    ],
                    w_ref[at : at + near, :],
                    preferred_element_type=F32,
                )
                total = term if total is None else total + term
        z_ref[loop] = total * (1.0 / width)


def chain_kernel(owner, loop, where, f_ref, z_ref, q_ref, rinv_ref, dv_ref, *refs):
    out_ref = refs[-1]

    @pl.when(where[0] == owner)
    def _():
        dv = dv_ref[...]
        wide = dv.astype(F32)
        pulled = lax.dot_general(dv, f_ref[loop], (((1,), (1,)), ((), ())), preferred_element_type=F32)
        along = jnp.sum(wide * z_ref[loop], axis=-1, keepdims=True)
        rinv = rinv_ref[loop][:, :1]
        out_ref[...] = (wide + rinv * (pulled - q_ref[loop] * along)).astype(BF16)


def change_kernel(loop, where, w_ref, x_ref, g_ref, *refs):
    dv_ref, dh_ref = refs[-2:]
    npipe = x_ref.shape[1] // refs[-3].shape[0]
    given = refs[:npipe]
    pieces = refs[-2 - npipe : -2]
    tok = x_ref.shape[1]
    if dv_ref.shape[0] > tok:
        dv_ref[tok:, :] = refs[npipe][...]
    section = where[0]
    for place in range(npipe):

        @pl.when(section == place)
        def _():
            dv_ref[:tok, :] = given[place][...]

    dh_ref[...] = lax.dot_general(
        dv_ref[:tok, :], w_ref[...], (((1,), (1,)), ((), ())), preferred_element_type=F32
    )
    share = tok // npipe
    for shift in range(npipe):
        start = lax.rem(section + shift, npipe) * share
        for at in range(0, share, CHUNK):
            rows = pl.ds(pl.multiple_of(start + at, CHUNK), CHUNK)
            x = x_ref[loop, rows, :].astype(F32)
            dhg = dh_ref[rows, :] * g_ref[loop]
            rinv = lax.rsqrt(jnp.mean(x * x, axis=-1, keepdims=True) + 1e-05)
            normed = x * rinv
            along = jnp.mean(dhg * normed, axis=-1, keepdims=True)
            pieces[shift][at : at + CHUNK, :] = (rinv * (dhg - normed * along)).astype(BF16)


def part_kernel(*refs):
    part_ref = refs[-1]
    count = (len(refs) - 2) // 2
    total = None
    for tiles_ref, dv_ref in zip(refs[:count], refs[count:-2], strict=True):
        tok = tiles_ref.shape[1]
        for loop in range(2):
            at = 0 if loop == 0 else tok
            term = lax.dot_general(
                tiles_ref[loop],
                dv_ref[at : at + tok, :],
                (((0,), (0,)), ((), ())),
                preferred_element_type=F32,
            )
            total = term if total is None else total + term
    part_ref[...] = total.astype(BF16)


def total_kernel(first, npipe, where, start_ref, *refs):
    given = refs[:npipe]
    run_ref, mark_ref = refs[-2:]
    results = refs[-2 - npipe : -2]
    mark_ref[...] = jnp.zeros_like(mark_ref)
    owner = where[0]
    share = run_ref.shape[0]
    for place in range(npipe):

        @pl.when(owner == place)
        def _():
            for at in range(0, share, CHUNK):
                base = place * share + at if first else at
                total = start_ref[base : base + CHUNK, :].astype(F32)
                for source in reversed(range(npipe)):
                    total = total + given[(place - source) % npipe][at : at + CHUNK, :].astype(F32)
                    results[(source - place) % npipe][at : at + CHUNK, :] = total.astype(BF16)
                run_ref[at : at + CHUNK, :] = total


def collect_kernel(npipe, where, *refs):
    *pieces, out_ref, sems = refs
    section = where[0]
    share = pieces[0].shape[0]
    copies = []
    for index, piece in enumerate(pieces):
        loop, shift = divmod(index, npipe)
        row = pl.multiple_of(lax.rem(section + npipe - shift, npipe) * share, share)
        target = out_ref.at[loop, pl.ds(row, share), :]
        copies.append(pltpu.make_async_copy(piece, target, sems.at[index]))
    for copy in copies:
        copy.start()
    for copy in copies:
        copy.wait()


def exchanged(pieces, axis):
    count = lax.axis_size(axis)
    moved = [pieces[0]]
    for shift in range(1, count):
        pairs = [(source, (source + shift) % count) for source in range(count)]
        moved.append(lax.ppermute(pieces[shift], axis, pairs))
    return moved


def on_device(saved, grad_out, gain, w_value):
    npipe = lax.axis_size("pipe")
    where = jnp.stack([lax.axis_index(name) for name in ("pipe", "dp_1", "dp_3")]).astype(jnp.int32)
    x = saved[:, 0]
    _, tok, width = x.shape
    kv_width = w_value.shape[2]
    share = tok // npipe
    far, across = lax.axis_size("dp_0"), lax.axis_size("dp_1")
    shape = jax.ShapeDtypeStruct

    mine = copy_for_each(w_value[0], DP[:3])
    other = lax.ppermute(mine, DP[3], [(0, 1), (1, 0)])
    tiles, fold_x, rinv, dv_first = kernel_call(
        norm_kernel,
        "normalize",
        (
            shape((across, 2, tok, width // across), BF16),
            shape((2, tok, kv_width), F32),
            shape((2, tok, HEAD), F32),
            shape((tok, kv_width), BF16),
        ),
        [IN_SMEM] + [IN_VMEM] * 3,
        (where, x, gain, grad_out),
    )
    gain_col = gain[:, 0].T
    w_mat, fold_w, along = kernel_call(
        fold_kernel,
        "fold_weights",
        (
            shape((width, kv_width), BF16),
            shape((2, kv_width, kv_width), BF16),
            shape((2, tok, kv_width), F32),
        ),
        [IN_SMEM] + [IN_VMEM] * 4,
        (where, mine, other, gain_col, tiles),
    )

    def changes(loop, given, after):
        out = kernel_call(
            functools.partial(change_kernel, loop),
            "changes",
            (shape((share, width), BF16),) * npipe
            + (shape(((2 - loop) * tok, kv_width), BF16),),
            [IN_SMEM] + [IN_VMEM] * (3 + npipe + len(after)),
            (where, w_mat, x, gain, *given, *after),
            scratch=(pltpu.VMEM((tok, width), F32),),
        )
        return out[:npipe], out[npipe]

    def totals(first, start, pieces, after):
        out = kernel_call(
            functools.partial(total_kernel, first, npipe),
            "totals",
            (shape((share, width), BF16),) * npipe
            + (shape((share, width), F32), shape((8, HEAD), F32)),
            [IN_SMEM] + [IN_VMEM] * (1 + npipe + len(after)),
            (where, start, *pieces, *after),
        )
        return out[:npipe], out[npipe], out[npipe + 1]

    arrived = [dv_first]
    dvs = [None, None]
    made = [None, None]
    back = [None, None]
    run = grad_out
    after, mark, behind = (), (), ()
    for hop in range(2 * npipe):
        owner, loop = npipe - 1 - hop % npipe, 1 - hop // npipe
        if hop < 2 * npipe - 1:
            following = kernel_call(
                functools.partial(chain_kernel, owner, loop),
                "chain",
                shape((tok, kv_width), BF16),
                [IN_SMEM] + [IN_VMEM] * (5 + len(after)),
                (where, fold_w, along, fold_x, rinv, arrived[hop], *after),
            )
            if hop == 0:
                hidden = exchanged(held_until(tiles, following), "dp_1")
            arrived.append(lax.ppermute(following, "pipe", [(owner, (owner - 1) % npipe)]))
        if owner == 0:
            given = [arrived[hop - place] for place in range(npipe)]
            made[loop], dvs[loop] = changes(loop, given, mark)
            behind = () if loop == 1 else tuple(back[1][1:])
            sums, run, sign = totals(loop == 1, run, exchanged(made[loop], "pipe"), behind)
            if loop == 0:
                spread = exchanged([dvs[0]] * across, "dp_1")
                part = kernel_call(
                    part_kernel,
                    "part",
                    shape((width // across, kv_width), BF16),
                    [IN_VMEM] * (2 * across + 1),
                    (*hidden, *spread, sign),
                )
            after, mark = (dvs[loop],), (dvs[loop], sign)
            back[loop] = exchanged(sums, "pipe")

    grad_x = kernel_call(
        functools.partial(collect_kernel, npipe),
        "collect_rows",
        shape((2, tok, width), BF16),
        [IN_SMEM] + [IN_VMEM] * (2 * npipe),
        (where, *back[0], *back[1]),
        scratch=(pltpu.SemaphoreType.DMA((2 * npipe,)),),
        out_spec=ANYWHERE,
    )[:, None]

    others = ("dp_0", "dp_2", "dp_3")
    pieces = part.reshape(lax.axis_size(others), -1, kv_width)
    landed = lax.all_to_all(pieces, others, 0, 0, tiled=True)
    grad_w = landed.astype(F32).sum(axis=0)[None]
    return (grad_x, grad_w)


def solution(mesh):
    finer = Mesh(
        mesh.devices.reshape(mesh.shape["pipe"], 2, 4, 4, 2),
        ("pipe", "dp_0", "dp_1", "dp_2", "dp_3"),
    )
    placed = (P(None, "pipe", DP, None), P(DP, None), P(None, "pipe", None), P("pipe", DP, None))
    return jax.shard_map(
        on_device,
        mesh=finer,
        in_specs=placed,
        out_specs=(P(None, "pipe", DP, None), P("pipe", DP, None)),
        check_vma=False,
    )
```

```python
import functools

import jax
import jax.numpy as jnp
from jax import lax
from jax.experimental import pallas as pl
from jax.experimental.pallas import tpu as pltpu
from jax.sharding import Mesh
from jax.sharding import PartitionSpec as P

HEAD = 128
CHUNK = 16
DP = ("dp_0", "dp_1", "dp_2", "dp_3")
IN_VMEM = pl.BlockSpec(memory_space=pltpu.VMEM)
IN_SMEM = pl.BlockSpec(memory_space=pltpu.SMEM)
ANYWHERE = pl.BlockSpec(memory_space=pl.ANY)
BF16, F32 = jnp.bfloat16, jnp.float32


def copy_for_each(array, axis):
    count = lax.axis_size(axis)
    return lax.all_to_all(
        jnp.broadcast_to(array[None], (count, *array.shape)), axis, 0, 0, tiled=True
    )


def kernel_call(kernel, name, out_shape, specs, operands, scratch=(), out_spec=IN_VMEM, room=8):
    return pl.pallas_call(
        kernel,
        out_shape=out_shape,
        in_specs=specs,
        out_specs=jax.tree.map(lambda _: out_spec, out_shape),
        scratch_shapes=list(scratch),
        compiler_params=pltpu.CompilerParams(vmem_limit_bytes=room * 2**20),
        name=name,
    )(*operands)


def held_until(value, token):
    return pl.pallas_call(
        lambda value_ref, token_ref, out_ref: None,
        out_shape=jax.ShapeDtypeStruct(value.shape, value.dtype),
        in_specs=[ANYWHERE, IN_VMEM],
        out_specs=ANYWHERE,
        input_output_aliases={0: 0},
        compiler_params=pltpu.CompilerParams(vmem_limit_bytes=2**20),
        name="held_until",
    )(value, token)


def folded(values, kv_width):
    group = values.shape[1] // kv_width
    sums = []
    for head in range(kv_width // HEAD):
        base = head * group * HEAD
        total = values[:, base : base + HEAD]
        for member in range(1, group):
            at = base + member * HEAD
            total = total + values[:, at : at + HEAD]
        sums.append(total)
    return jnp.concatenate(sums, axis=1)


def norm_kernel(where, x_ref, g_ref, fresh_ref, tiles_ref, q_ref, rinv_ref, dv_ref):
    _, tok, width = x_ref.shape
    kv_width = dv_ref.shape[1]
    across, _, _, part = tiles_ref.shape
    far = 2
    near = part // far

    def one(index, carry):
        row = pl.multiple_of(index * CHUNK, CHUNK)
        rows = pl.ds(row, CHUNK)
        dv_ref[rows, :] = folded(fresh_ref[rows, :].astype(F32), kv_width).astype(BF16)
        for loop in range(2):
            x = x_ref[loop, rows, :].astype(F32)
            rinv = lax.rsqrt(jnp.mean(x * x, axis=-1, keepdims=True) + 1e-05)
            normed = x * rinv
            rinv_ref[loop, rows, :] = jnp.broadcast_to(rinv, (CHUNK, HEAD))
            q_ref[loop, rows, :] = folded(normed, kv_width)
            hidden = (normed * g_ref[loop]).astype(BF16)
            for place in range(across):
                for half in range(far):
                    at = (half * across + place) * near
                    tiles_ref[lax.rem(place + across - where[1], across), loop, rows, half * near : (half + 1) * near] = hidden[
                        :, at : at + near
                    ]
        return carry

    lax.fori_loop(0, tok // CHUNK, one, 0)


def fold_kernel(where, mine_ref, other_ref, gcol_ref, tiles_ref, w_ref, f_ref, z_ref):
    width, kv_width = w_ref.shape
    count, piece, _ = mine_ref.shape
    for index in range(count):
        for ref, core in ((mine_ref, where[2]), (other_ref, 1 - where[2])):
            at = pl.multiple_of((2 * index + core) * piece, piece)
            w_ref[pl.ds(at, piece), :] = ref[index]
    across, _, tok, part = tiles_ref.shape
    far = 2
    near = part // far
    group = width // kv_width
    for head in range(kv_width // HEAD):
        for row in range(0, HEAD, CHUNK):
            totals = [None, None]
            for member in range(group):
                at = (head * group + member) * HEAD + row
                rows = w_ref[at : at + CHUNK, :].astype(F32)
                for loop in range(2):
                    term = rows * gcol_ref[at : at + CHUNK, loop : loop + 1]
                    totals[loop] = term if member == 0 else totals[loop] + term
            for loop in range(2):
                f_ref[loop, head * HEAD + row : head * HEAD + row + CHUNK, :] = totals[loop].astype(BF16)
    for loop in range(2):
        total = None
        for place in range(across):
            for half in range(far):
                at = (half * across + place) * near
                term = jnp.dot(
                    tiles_ref[
                        lax.rem(place + across - where[1], across),
                        loop,
                        :,
                        half * near : (half + 1) * near,
                    ],
                    w_ref[at : at + near, :],
                    preferred_element_type=F32,
                )
                total = term if total is None else total + term
        z_ref[loop] = total * (1.0 / width)


def chain_kernel(owner, loop, where, f_ref, z_ref, q_ref, rinv_ref, dv_ref, *refs):
    out_ref = refs[-1]

    @pl.when(where[0] == owner)
    def _():
        dv = dv_ref[...]
        wide = dv.astype(F32)
        pulled = lax.dot_general(dv, f_ref[loop], (((1,), (1,)), ((), ())), preferred_element_type=F32)
        along = jnp.sum(wide * z_ref[loop], axis=-1, keepdims=True)
        rinv = rinv_ref[loop][:, :1]
        out_ref[...] = (wide + rinv * (pulled - q_ref[loop] * along)).astype(BF16)


def change_kernel(loop, where, w_ref, x_ref, g_ref, *refs):
    dv_ref, dh_ref = refs[-2:]
    npipe = x_ref.shape[1] // refs[-3].shape[0]
    given = refs[:npipe]
    pieces = refs[-2 - npipe : -2]
    tok = x_ref.shape[1]
    if dv_ref.shape[0] > tok:
        dv_ref[tok:, :] = refs[npipe][...]
    section = where[0]
    for place in range(npipe):

        @pl.when(section == place)
        def _():
            dv_ref[:tok, :] = given[place][...]

    dh_ref[...] = lax.dot_general(
        dv_ref[:tok, :], w_ref[...], (((1,), (1,)), ((), ())), preferred_element_type=F32
    )
    share = tok // npipe
    for shift in range(npipe):
        start = lax.rem(section + shift, npipe) * share
        for at in range(0, share, CHUNK):
            rows = pl.ds(pl.multiple_of(start + at, CHUNK), CHUNK)
            x = x_ref[loop, rows, :].astype(F32)
            dhg = dh_ref[rows, :] * g_ref[loop]
            rinv = lax.rsqrt(jnp.mean(x * x, axis=-1, keepdims=True) + 1e-05)
            normed = x * rinv
            along = jnp.mean(dhg * normed, axis=-1, keepdims=True)
            pieces[shift][at : at + CHUNK, :] = (rinv * (dhg - normed * along)).astype(BF16)


def part_kernel(*refs):
    part_ref = refs[-1]
    count = (len(refs) - 2) // 2
    total = None
    for tiles_ref, dv_ref in zip(refs[:count], refs[count:-2], strict=True):
        tok = tiles_ref.shape[1]
        for loop in range(2):
            at = 0 if loop == 0 else tok
            term = lax.dot_general(
                tiles_ref[loop],
                dv_ref[at : at + tok, :],
                (((0,), (0,)), ((), ())),
                preferred_element_type=F32,
            )
            total = term if total is None else total + term
    part_ref[...] = total.astype(BF16)


def total_kernel(npipe, where, start_ref, *refs):
    given, results = refs[: 2 * npipe], refs[2 * npipe :]
    owner = where[0]
    share = given[0].shape[0]
    for place in range(npipe):

        @pl.when(owner == place)
        def _():
            for at in range(0, share, CHUNK):
                base = place * share + at
                rows = slice(at, at + CHUNK)
                total = start_ref[base : base + CHUNK, :].astype(F32)
                for loop in (1, 0):
                    for source in reversed(range(npipe)):
                        piece = given[(1 - loop) * npipe + (place - source) % npipe]
                        total = total + piece[rows, :].astype(F32)
                        results[(source - place) % npipe][loop, rows, :] = total.astype(BF16)


def collect_kernel(npipe, where, *refs):
    *pieces, out_ref, sems = refs
    section = where[0]
    share = pieces[0].shape[1]
    copies = []
    for shift, piece in enumerate(pieces):
        row = pl.multiple_of(lax.rem(section + npipe - shift, npipe) * share, share)
        for loop in range(2):
            target = out_ref.at[loop, pl.ds(row, share), :]
            copies.append(pltpu.make_async_copy(piece.at[loop], target, sems.at[2 * shift + loop]))
    for copy in copies:
        copy.start()
    for copy in copies:
        copy.wait()


def exchanged(pieces, axis):
    count = lax.axis_size(axis)
    moved = [pieces[0]]
    for shift in range(1, count):
        pairs = [(source, (source + shift) % count) for source in range(count)]
        moved.append(lax.ppermute(pieces[shift], axis, pairs))
    return moved


def on_device(saved, grad_out, gain, w_value):
    npipe = lax.axis_size("pipe")
    where = jnp.stack([lax.axis_index(name) for name in ("pipe", "dp_1", "dp_3")]).astype(jnp.int32)
    x = saved[:, 0]
    _, tok, width = x.shape
    kv_width = w_value.shape[2]
    share = tok // npipe
    far, across = lax.axis_size("dp_0"), lax.axis_size("dp_1")
    shape = jax.ShapeDtypeStruct

    mine = copy_for_each(w_value[0], DP[:3])
    other = lax.ppermute(mine, DP[3], [(0, 1), (1, 0)])
    tiles, fold_x, rinv, dv_first = kernel_call(
        norm_kernel,
        "normalize",
        (
            shape((across, 2, tok, width // across), BF16),
            shape((2, tok, kv_width), F32),
            shape((2, tok, HEAD), F32),
            shape((tok, kv_width), BF16),
        ),
        [IN_SMEM] + [IN_VMEM] * 3,
        (where, x, gain, grad_out),
    )
    gain_col = gain[:, 0].T
    w_mat, fold_w, along = kernel_call(
        fold_kernel,
        "fold_weights",
        (
            shape((width, kv_width), BF16),
            shape((2, kv_width, kv_width), BF16),
            shape((2, tok, kv_width), F32),
        ),
        [IN_SMEM] + [IN_VMEM] * 4,
        (where, mine, other, gain_col, tiles),
    )

    def changes(loop, given, after, later):
        out = kernel_call(
            functools.partial(change_kernel, loop),
            "changes",
            (shape((share, width), BF16),) * npipe
            + (shape(((2 - loop) * tok, kv_width), BF16),),
            [IN_SMEM] + [IN_VMEM] * (3 + npipe + len(after)) + [ANYWHERE] * len(later),
            (where, w_mat, x, gain, *given, *after, *later),
            scratch=(pltpu.VMEM((tok, width), F32),),
        )
        return out[:npipe], out[npipe]

    arrived = [dv_first]
    dvs = [None, None]
    moved = [None, None]
    for hop in range(2 * npipe):
        owner, loop = npipe - 1 - hop % npipe, 1 - hop // npipe
        after = ()
        if hop == npipe:
            after = (dvs[1],)
        elif hop == 2 * npipe - 2:
            after = tuple(moved[1][1:])
        if hop < 2 * npipe - 1:
            following = kernel_call(
                functools.partial(chain_kernel, owner, loop),
                "chain",
                shape((tok, kv_width), BF16),
                [IN_SMEM] + [IN_VMEM] * (5 + len(after)),
                (where, fold_w, along, fold_x, rinv, arrived[hop], *after),
            )
            if hop == 0:
                hidden = exchanged(held_until(tiles, following), "dp_1")
            arrived.append(lax.ppermute(following, "pipe", [(owner, (owner - 1) % npipe)]))
        if owner == 0:
            given = [arrived[hop - place] for place in range(npipe)]
            before = () if loop == 1 else (dvs[1],)
            made, dvs[loop] = changes(loop, given, before, hidden[1:] if loop == 1 else ())
            moved[loop] = exchanged(made, "pipe")
    sums = kernel_call(
        functools.partial(total_kernel, npipe),
        "totals",
        (shape((2, share, width), BF16),) * npipe,
        [IN_SMEM] + [IN_VMEM] * (1 + 2 * npipe),
        (where, grad_out, *moved[1], *moved[0]),
    )
    back = exchanged(sums, "pipe")
    grad_x = kernel_call(
        functools.partial(collect_kernel, npipe),
        "collect_rows",
        shape((2, tok, width), BF16),
        [IN_SMEM] + [IN_VMEM] * npipe,
        (where, *back),
        scratch=(pltpu.SemaphoreType.DMA((2 * npipe,)),),
        out_spec=ANYWHERE,
    )[:, None]

    spread = exchanged([dvs[0]] * across, "dp_1")
    part = kernel_call(
        part_kernel,
        "part",
        shape((width // across, kv_width), BF16),
        [IN_VMEM] * (2 * across + 1),
        (*hidden, *spread, sums[0]),
    )
    others = ("dp_0", "dp_2", "dp_3")
    pieces = part.reshape(lax.axis_size(others), -1, kv_width)
    landed = lax.all_to_all(pieces, others, 0, 0, tiled=True)
    grad_w = landed.astype(F32).sum(axis=0)[None]
    return (grad_x, grad_w)


def solution(mesh):
    finer = Mesh(
        mesh.devices.reshape(mesh.shape["pipe"], 2, 4, 4, 2),
        ("pipe", "dp_0", "dp_1", "dp_2", "dp_3"),
    )
    placed = (P(None, "pipe", DP, None), P(DP, None), P(None, "pipe", None), P("pipe", DP, None))
    return jax.shard_map(
        on_device,
        mesh=finer,
        in_specs=placed,
        out_specs=(P(None, "pipe", DP, None), P("pipe", DP, None)),
        check_vma=False,
    )
```

```python
import functools

import jax
import jax.numpy as jnp
from jax import lax
from jax.experimental import pallas as pl
from jax.experimental.pallas import tpu as pltpu
from jax.sharding import Mesh
from jax.sharding import PartitionSpec as P

HEAD = 128
ROWS = 16
SLACK = 2
FAR = 2
HIDDEN_BY = 11
DP = ("dp_0", "dp_1", "dp_2", "dp_3")
IN_VMEM = pl.BlockSpec(memory_space=pltpu.VMEM)
IN_SMEM = pl.BlockSpec(memory_space=pltpu.SMEM)
ANYWHERE = pl.BlockSpec(memory_space=pl.ANY)
BF16, F32 = jnp.bfloat16, jnp.float32


def copy_for_each(array, axis):
    count = lax.axis_size(axis)
    return lax.all_to_all(
        jnp.broadcast_to(array[None], (count, *array.shape)), axis, 0, 0, tiled=True
    )


def kernel_call(kernel, name, out_shape, specs, operands, scratch=(), out_spec=IN_VMEM, room=8):
    return pl.pallas_call(
        kernel,
        out_shape=out_shape,
        in_specs=specs,
        out_specs=jax.tree.map(lambda _: out_spec, out_shape),
        scratch_shapes=list(scratch),
        compiler_params=pltpu.CompilerParams(vmem_limit_bytes=room * 2**20),
        name=name,
    )(*operands)


def held_until(value, token):
    return pl.pallas_call(
        lambda value_ref, token_ref, out_ref: None,
        out_shape=jax.ShapeDtypeStruct(value.shape, value.dtype),
        in_specs=[ANYWHERE, IN_VMEM],
        out_specs=ANYWHERE,
        input_output_aliases={0: 0},
        compiler_params=pltpu.CompilerParams(vmem_limit_bytes=2**20),
        name="held_until",
    )(value, token)


def norm_kernel(where, x_ref, g_ref, tiles_ref):
    _, tok, width = x_ref.shape
    across, _, _, part = tiles_ref.shape
    near = width // (across * FAR)

    def one(index, carry):
        rows = pl.ds(pl.multiple_of(index * ROWS, ROWS), ROWS)
        for loop in range(2):
            x = x_ref[loop, rows, :].astype(F32)
            rinv = lax.rsqrt(jnp.mean(x * x, axis=-1, keepdims=True) + 1e-05)
            hidden = (x * rinv * g_ref[loop]).astype(BF16)
            for place in range(across):
                for half in range(FAR):
                    at = (half * across + place) * near
                    tiles_ref[
                        lax.rem(place + across - where[1], across),
                        loop,
                        rows,
                        half * near : (half + 1) * near,
                    ] = hidden[:, at : at + near]
        return carry

    lax.fori_loop(0, tok // ROWS, one, 0)


def rows_kernel(where, mine_ref, other_ref, w_ref):
    count, piece, _ = mine_ref.shape
    for index in range(count):
        for ref, core in ((mine_ref, where[2]), (other_ref, 1 - where[2])):
            at = pl.multiple_of((2 * index + core) * piece, piece)
            w_ref[pl.ds(at, piece), :] = ref[index]


def part_kernel(*refs):
    part_ref = refs[-1]
    count = (len(refs) - 1) // 2
    total = None
    for tiles_ref, dv_ref in zip(refs[:count], refs[count:-1], strict=True):
        tok = tiles_ref.shape[1]
        for loop in range(2):
            at = 0 if loop == 0 else tok
            term = lax.dot_general(
                tiles_ref[loop],
                dv_ref[at : at + tok, :],
                (((0,), (0,)), ((), ())),
                preferred_element_type=F32,
            )
            total = term if total is None else total + term
    part_ref[...] = total.astype(BF16)


def task_of(step, section, npipe):
    return step - SLACK * (npipe - 1 - section)


def step_kernel(step, npipe, blocks, where, w_ref, x_ref, g_ref, fresh_ref, in_ref, *refs):
    dx_ref, dv_ref = refs[-2:]
    section = where[0]
    task = task_of(step, section, npipe)

    @pl.when((task >= 0) & (task < 2 * blocks))
    def _():
        later = task < blocks
        loop = jnp.where(later, 1, 0)
        block = jnp.where(later, task, task - blocks)
        row = pl.multiple_of(block * ROWS, ROWS)
        width = dx_ref.shape[1]
        kv_width = dv_ref.shape[1]
        heads = kv_width // HEAD
        group = width // kv_width
        take = later & (section == npipe - 1)
        dy = jnp.where(take, fresh_ref[pl.ds(row, ROWS), :], in_ref[...]).astype(F32)
        x = x_ref[loop, pl.ds(row, ROWS), :].astype(F32)
        sums = []
        for head in range(heads):
            base = head * group * HEAD
            total = dy[:, base : base + HEAD]
            for member in range(1, group):
                at = base + member * HEAD
                total = total + dy[:, at : at + HEAD]
            sums.append(total)
        dv = jnp.concatenate(sums, axis=1).astype(BF16)
        dv_ref[...] = dv
        dh = lax.dot_general(
            dv, w_ref[...], (((1,), (1,)), ((), ())), preferred_element_type=F32
        )
        dhg = dh * g_ref[loop]
        rinv = lax.rsqrt(jnp.mean(x * x, axis=-1, keepdims=True) + 1e-05)
        normed = x * rinv
        along = jnp.mean(dhg * normed, axis=-1, keepdims=True)
        dx_ref[...] = (dy + rinv * (dhg - normed * along)).astype(BF16)


def collect_kernel(npipe, blocks, where, *refs):
    *pieces, out_ref, sems = refs
    section = where[0]

    def each(act):
        for step, piece in enumerate(pieces):
            task = task_of(step, section, npipe)

            @pl.when((task >= 0) & (task < 2 * blocks))
            def _():
                later = task < blocks
                loop = jnp.where(later, 1, 0)
                row = pl.multiple_of((task - jnp.where(later, 0, blocks)) * ROWS, ROWS)
                target = out_ref.at[loop, pl.ds(row, ROWS), :]
                act(pltpu.make_async_copy(piece, target, sems.at[step]))

    each(lambda copy: copy.start())
    each(lambda copy: copy.wait())


def stack_kernel(npipe, blocks, where, *refs):
    *pieces, out_ref = refs
    section = where[0]
    for step, piece in enumerate(pieces):
        task = task_of(step, section, npipe)

        @pl.when((task >= 0) & (task < 2 * blocks))
        def _():
            place = task + jnp.where(task < blocks, blocks, -blocks)
            out_ref[pl.ds(pl.multiple_of(place * ROWS, ROWS), ROWS), :] = piece[...]


def exchanged(pieces, axis):
    count = lax.axis_size(axis)
    moved = [pieces[0]]
    for shift in range(1, count):
        pairs = [(source, (source + shift) % count) for source in range(count)]
        moved.append(lax.ppermute(pieces[shift], axis, pairs))
    return moved


def on_device(saved, grad_out, gain, w_value):
    npipe = lax.axis_size("pipe")
    where = jnp.stack([lax.axis_index(name) for name in ("pipe", "dp_1", "dp_3")]).astype(jnp.int32)
    x = saved[:, 0]
    _, tok, width = x.shape
    kv_width = w_value.shape[2]
    blocks = tok // ROWS
    across = lax.axis_size("dp_1")
    shape = jax.ShapeDtypeStruct

    mine = copy_for_each(w_value[0], DP[:3])
    other = lax.ppermute(mine, DP[3], [(0, 1), (1, 0)])
    tiles = kernel_call(
        norm_kernel,
        "normalize",
        shape((across, 2, tok, width // across), BF16),
        [IN_SMEM] + [IN_VMEM] * 2,
        (where, x, gain),
    )
    w_mat = kernel_call(
        rows_kernel,
        "rows",
        shape((width, kv_width), BF16),
        [IN_SMEM] + [IN_VMEM] * 2,
        (where, mine, other),
    )

    steps = 2 * blocks + SLACK * (npipe - 1)
    sent, gx_parts, gv_parts = {}, [], []
    for step in range(steps):
        incoming = sent.pop(step - SLACK, None)
        if incoming is None:
            incoming = jnp.zeros((ROWS, width), BF16)
        later = tuple(hidden[1:]) if step == HIDDEN_BY else ()
        dx, dv = kernel_call(
            functools.partial(step_kernel, step, npipe, blocks),
            "section_step",
            (shape((ROWS, width), BF16), shape((ROWS, kv_width), BF16)),
            [IN_SMEM] + [IN_VMEM] * (5 + min(step, 1)) + [ANYWHERE] * len(later),
            (where, w_mat, x, gain, grad_out, incoming, *gv_parts[-1:], *later),
        )
        gx_parts.append(dx)
        gv_parts.append(dv)
        pairs = []
        for source in range(npipe):
            task = task_of(step, source, npipe)
            if 0 <= task < (blocks if source == 0 else 2 * blocks):
                pairs.append((source, (source - 1) % npipe))
        if pairs:
            sent[step] = lax.ppermute(dx, "pipe", pairs)
        if step == 4:
            hidden = exchanged(held_until(tiles, dv), "dp_1")

    grad_x = kernel_call(
        functools.partial(collect_kernel, npipe, blocks),
        "collect_rows",
        shape((2, tok, width), BF16),
        [IN_SMEM] + [IN_VMEM] * steps,
        (where, *gx_parts),
        scratch=(pltpu.SemaphoreType.DMA((steps,)),),
        out_spec=ANYWHERE,
    )[:, None]
    dv_all = kernel_call(
        functools.partial(stack_kernel, npipe, blocks),
        "stack",
        shape((2 * tok, kv_width), BF16),
        [IN_SMEM] + [IN_VMEM] * steps,
        (where, *gv_parts),
    )
    spread = exchanged([dv_all] * across, "dp_1")
    part = kernel_call(
        part_kernel,
        "part",
        shape((width // across, kv_width), BF16),
        [IN_VMEM] * (2 * across),
        (*hidden, *spread),
    )
    others = ("dp_0", "dp_2", "dp_3")
    pieces = part.reshape(lax.axis_size(others), -1, kv_width)
    landed = lax.all_to_all(pieces, others, 0, 0, tiled=True)
    grad_w = landed.astype(F32).sum(axis=0)[None]
    return (grad_x, grad_w)


def solution(mesh):
    finer = Mesh(
        mesh.devices.reshape(mesh.shape["pipe"], 2, 4, 4, 2),
        ("pipe", "dp_0", "dp_1", "dp_2", "dp_3"),
    )
    placed = (P(None, "pipe", DP, None), P(DP, None), P(None, "pipe", None), P("pipe", DP, None))
    return jax.shard_map(
        on_device,
        mesh=finer,
        in_specs=placed,
        out_specs=(P(None, "pipe", DP, None), P("pipe", DP, None)),
        check_vma=False,
    )
```

```python
import functools

import jax
import jax.numpy as jnp
from jax import lax
from jax.experimental import pallas as pl
from jax.experimental.pallas import tpu as pltpu
from jax.sharding import Mesh
from jax.sharding import PartitionSpec as P

HEAD = 128
ROWS = 16
SLACK = 2
FAR = 2
HIDDEN_AT = 7
HIDDEN_BY = 12
PART_AT = 20
DP = ("dp_0", "dp_1", "dp_2", "dp_3")
IN_VMEM = pl.BlockSpec(memory_space=pltpu.VMEM)
IN_SMEM = pl.BlockSpec(memory_space=pltpu.SMEM)
ANYWHERE = pl.BlockSpec(memory_space=pl.ANY)
BF16, F32 = jnp.bfloat16, jnp.float32


def copy_for_each(array, axis):
    count = lax.axis_size(axis)
    return lax.all_to_all(
        jnp.broadcast_to(array[None], (count, *array.shape)), axis, 0, 0, tiled=True
    )


def kernel_call(kernel, name, out_shape, specs, operands, scratch=(), out_spec=IN_VMEM, room=8):
    return pl.pallas_call(
        kernel,
        out_shape=out_shape,
        in_specs=specs,
        out_specs=jax.tree.map(lambda _: out_spec, out_shape),
        scratch_shapes=list(scratch),
        compiler_params=pltpu.CompilerParams(vmem_limit_bytes=room * 2**20),
        name=name,
    )(*operands)


def held_until(value, token):
    return pl.pallas_call(
        lambda value_ref, token_ref, out_ref: None,
        out_shape=jax.ShapeDtypeStruct(value.shape, value.dtype),
        in_specs=[ANYWHERE, IN_VMEM],
        out_specs=ANYWHERE,
        input_output_aliases={0: 0},
        compiler_params=pltpu.CompilerParams(vmem_limit_bytes=2**20),
        name="held_until",
    )(value, token)


def folded(values, kv_width):
    group = values.shape[1] // kv_width
    sums = []
    for head in range(kv_width // HEAD):
        base = head * group * HEAD
        total = values[:, base : base + HEAD]
        for member in range(1, group):
            at = base + member * HEAD
            total = total + values[:, at : at + HEAD]
        sums.append(total)
    return jnp.concatenate(sums, axis=1)


def norm_kernel(where, x_ref, g_ref, tiles_ref):
    _, tok, width = x_ref.shape
    across, _, _, part = tiles_ref.shape
    near = width // (across * FAR)

    def one(index, carry):
        rows = pl.ds(pl.multiple_of(index * ROWS, ROWS), ROWS)
        for loop in range(2):
            x = x_ref[loop, rows, :].astype(F32)
            rinv = lax.rsqrt(jnp.mean(x * x, axis=-1, keepdims=True) + 1e-05)
            hidden = (x * rinv * g_ref[loop]).astype(BF16)
            for place in range(across):
                for half in range(FAR):
                    at = (half * across + place) * near
                    tiles_ref[
                        lax.rem(place + across - where[1], across),
                        loop,
                        rows,
                        half * near : (half + 1) * near,
                    ] = hidden[:, at : at + near]
        return carry

    lax.fori_loop(0, tok // ROWS, one, 0)


def rows_kernel(where, mine_ref, other_ref, w_ref):
    count, piece, _ = mine_ref.shape
    for index in range(count):
        for ref, core in ((mine_ref, where[2]), (other_ref, 1 - where[2])):
            at = pl.multiple_of((2 * index + core) * piece, piece)
            w_ref[pl.ds(at, piece), :] = ref[index]


def part_kernel(*refs):
    part_ref = refs[-1]
    count = (len(refs) - 4) // 2
    total = None
    for tiles_ref, dv_ref in zip(refs[:count], refs[count:-4], strict=True):
        tok = tiles_ref.shape[1]
        for loop in range(2):
            at = 0 if loop == 0 else tok
            term = lax.dot_general(
                tiles_ref[loop],
                dv_ref[at : at + tok, :],
                (((0,), (0,)), ((), ())),
                preferred_element_type=F32,
            )
            total = term if total is None else total + term
    part_ref[...] = total.astype(BF16)


def task_of(step, section, npipe):
    return step - SLACK * (npipe - 1 - section)


def change_kernel(owner, loop, first, where, w_ref, x_ref, g_ref, from_ref, *refs):
    *outs, dh_ref = refs
    change_ref, next_ref = outs[-3:-1] if first else outs[-2:]
    dv_ref = outs[-1] if first else from_ref

    @pl.when(where[0] == owner)
    def _():
        tok, kv_width = next_ref.shape
        if first:
            for at in range(0, tok, ROWS):
                rows = slice(at, at + ROWS)
                dv_ref[rows, :] = folded(from_ref[rows, :].astype(F32), kv_width).astype(BF16)
        dh_ref[...] = lax.dot_general(
            dv_ref[...], w_ref[...], (((1,), (1,)), ((), ())), preferred_element_type=F32
        )
        for at in range(0, tok, ROWS):
            rows = slice(at, at + ROWS)
            x = x_ref[loop, rows, :].astype(F32)
            dhg = dh_ref[rows, :] * g_ref[loop]
            rinv = lax.rsqrt(jnp.mean(x * x, axis=-1, keepdims=True) + 1e-05)
            normed = x * rinv
            along = jnp.mean(dhg * normed, axis=-1, keepdims=True)
            change = rinv * (dhg - normed * along)
            change_ref[rows, :] = change.astype(BF16)
            next_ref[rows, :] = (dv_ref[rows, :].astype(F32) + folded(change, kv_width)).astype(BF16)


def step_kernel(tasks, blocks, where, fresh_ref, in_ref, *refs):
    dx_ref = refs[-1]
    for place, task in enumerate(tasks):
        if task is None:
            continue

        @pl.when(where[0] == place)
        def _():
            at = task % blocks * ROWS
            rows = slice(at, at + ROWS)
            fresh = place == len(tasks) - 1 and task < blocks
            dy = fresh_ref[rows, :] if fresh else in_ref[...]
            dx_ref[...] = (dy.astype(F32) + refs[place][rows, :].astype(F32)).astype(BF16)


def collect_kernel(npipe, blocks, where, *refs):
    *pieces, out_ref, sems = refs
    section = where[0]

    def each(act):
        for step, piece in enumerate(pieces):
            task = task_of(step, section, npipe)

            @pl.when((task >= 0) & (task < 2 * blocks))
            def _():
                later = task < blocks
                loop = jnp.where(later, 1, 0)
                row = pl.multiple_of((task - jnp.where(later, 0, blocks)) * ROWS, ROWS)
                target = out_ref.at[loop, pl.ds(row, ROWS), :]
                act(pltpu.make_async_copy(piece, target, sems.at[step]))

    each(lambda copy: copy.start())
    each(lambda copy: copy.wait())


def stack_kernel(npipe, where, *refs):
    out_ref = refs[-1]
    tok = refs[0].shape[0]
    for place in range(npipe):

        @pl.when(where[0] == place)
        def _():
            out_ref[tok:, :] = refs[npipe - 1 - place][...]
            out_ref[:tok, :] = refs[2 * npipe - 1 - place][...]


def exchanged(pieces, axis):
    count = lax.axis_size(axis)
    moved = [pieces[0]]
    for shift in range(1, count):
        pairs = [(source, (source + shift) % count) for source in range(count)]
        moved.append(lax.ppermute(pieces[shift], axis, pairs))
    return moved


def on_device(saved, grad_out, gain, w_value):
    npipe = lax.axis_size("pipe")
    where = jnp.stack([lax.axis_index(name) for name in ("pipe", "dp_1", "dp_3")]).astype(jnp.int32)
    x = saved[:, 0]
    _, tok, width = x.shape
    kv_width = w_value.shape[2]
    blocks = tok // ROWS
    across = lax.axis_size("dp_1")
    shape = jax.ShapeDtypeStruct

    mine = copy_for_each(w_value[0], DP[:3])
    other = lax.ppermute(mine, DP[3], [(0, 1), (1, 0)])
    tiles = kernel_call(
        norm_kernel,
        "normalize",
        shape((across, 2, tok, width // across), BF16),
        [IN_SMEM] + [IN_VMEM] * 2,
        (where, x, gain),
    )
    w_mat = kernel_call(
        rows_kernel,
        "rows",
        shape((width, kv_width), BF16),
        [IN_SMEM] + [IN_VMEM] * 2,
        (where, mine, other),
    )

    steps = 2 * blocks + SLACK * (npipe - 1)
    sent, gx_parts, arrived, changes = {}, [], [], []
    turn = []
    for step in range(steps):
        hop, odd = divmod(step, SLACK)
        if not odd and hop < 2 * npipe:
            owner, loop, first = npipe - 1 - hop % npipe, 1 - hop // npipe, hop == 0
            outs = (shape((tok, width), BF16), shape((tok, kv_width), BF16))
            source = grad_out if first else arrived[hop]
            out = kernel_call(
                functools.partial(change_kernel, owner, loop, first),
                "changes",
                outs + outs[1:] * first,
                [IN_SMEM] + [IN_VMEM] * (4 + len(turn)),
                (where, w_mat, x, gain, source, *turn),
                scratch=(pltpu.VMEM((tok, width), F32),),
            )
            changes.append(out[0])
            turn = [out[1]]
            if first:
                arrived.append(out[2])
            if hop < 2 * npipe - 1:
                arrived.append(lax.ppermute(out[1], "pipe", [(owner, (owner - 1) % npipe)]))
            else:
                dv_all = kernel_call(
                    functools.partial(stack_kernel, npipe),
                    "stack",
                    shape((2 * tok, kv_width), BF16),
                    [IN_SMEM] + [IN_VMEM] * (2 * npipe),
                    (where, *arrived),
                )
                spread = exchanged([dv_all] * across, "dp_1")
        incoming = sent.pop(step - SLACK, None)
        if incoming is None:
            incoming = grad_out[:ROWS]
        later = ()
        if step == PART_AT - 1:
            before = incoming
        if step == HIDDEN_BY:
            later = tuple(hidden[1:])
        elif step == PART_AT:
            part = kernel_call(
                part_kernel,
                "part",
                shape((width // across, kv_width), BF16),
                [IN_VMEM] * (2 * across + 3),
                (*hidden, *spread, incoming, before, *turn),
            )
        tasks, pairs, mine_of = [], [], []
        for place in range(npipe):
            task = task_of(step, place, npipe)
            valid = 0 <= task < 2 * blocks
            tasks.append(task if valid else None)
            source = npipe - 1 - place + (npipe if task >= blocks else 0)
            mine_of.append(changes[source if valid else 0])
            if valid and not (place == 0 and task >= blocks):
                pairs.append((place, (place - 1) % npipe))
        dx = kernel_call(
            functools.partial(step_kernel, tuple(tasks), blocks),
            "section_step",
            shape((ROWS, width), BF16),
            [IN_SMEM] + [IN_VMEM] * (2 + npipe + len(turn)) + [ANYWHERE] * len(later),
            (where, grad_out, incoming, *mine_of, *turn, *later),
        )
        gx_parts.append(dx)
        turn = [dx]
        if pairs:
            sent[step] = lax.ppermute(dx, "pipe", pairs)
        if step == HIDDEN_AT:
            hidden = exchanged(held_until(tiles, dx), "dp_1")

    grad_x = kernel_call(
        functools.partial(collect_kernel, npipe, blocks),
        "collect_rows",
        shape((2, tok, width), BF16),
        [IN_SMEM] + [IN_VMEM] * steps,
        (where, *gx_parts),
        scratch=(pltpu.SemaphoreType.DMA((steps,)),),
        out_spec=ANYWHERE,
    )[:, None]
    others = ("dp_0", "dp_2", "dp_3")
    pieces = part.reshape(lax.axis_size(others), -1, kv_width)
    landed = lax.all_to_all(pieces, others, 0, 0, tiled=True)
    grad_w = landed.astype(F32).sum(axis=0)[None]
    return (grad_x, grad_w)


def solution(mesh):
    finer = Mesh(
        mesh.devices.reshape(mesh.shape["pipe"], 2, 4, 4, 2),
        ("pipe", "dp_0", "dp_1", "dp_2", "dp_3"),
    )
    placed = (P(None, "pipe", DP, None), P(DP, None), P(None, "pipe", None), P("pipe", DP, None))
    return jax.shard_map(
        on_device,
        mesh=finer,
        in_specs=placed,
        out_specs=(P(None, "pipe", DP, None), P("pipe", DP, None)),
        check_vma=False,
    )
```

```python
import functools

import jax
import jax.numpy as jnp
from jax import lax
from jax.experimental import pallas as pl
from jax.experimental.pallas import tpu as pltpu
from jax.sharding import Mesh
from jax.sharding import PartitionSpec as P

HEAD = 128
ROWS = 16
SLACK = 2
FAR = 2
HIDDEN_AT = 5
HIDDEN_BY = 12
DP = ("dp_0", "dp_1", "dp_2", "dp_3")
IN_VMEM = pl.BlockSpec(memory_space=pltpu.VMEM)
IN_SMEM = pl.BlockSpec(memory_space=pltpu.SMEM)
ANYWHERE = pl.BlockSpec(memory_space=pl.ANY)
BF16, F32 = jnp.bfloat16, jnp.float32


def copy_for_each(array, axis):
    count = lax.axis_size(axis)
    return lax.all_to_all(
        jnp.broadcast_to(array[None], (count, *array.shape)), axis, 0, 0, tiled=True
    )


def kernel_call(kernel, name, out_shape, specs, operands, scratch=(), out_spec=IN_VMEM, room=8):
    return pl.pallas_call(
        kernel,
        out_shape=out_shape,
        in_specs=specs,
        out_specs=jax.tree.map(lambda _: out_spec, out_shape),
        scratch_shapes=list(scratch),
        compiler_params=pltpu.CompilerParams(vmem_limit_bytes=room * 2**20),
        name=name,
    )(*operands)


def norm_kernel(where, x_ref, g_ref, turn_ref, tiles_ref):
    _, tok, width = x_ref.shape
    across, _, _, part = tiles_ref.shape
    near = width // (across * FAR)

    def one(index, carry):
        rows = pl.ds(pl.multiple_of(index * ROWS, ROWS), ROWS)
        for loop in range(2):
            x = x_ref[loop, rows, :].astype(F32)
            rinv = lax.rsqrt(jnp.mean(x * x, axis=-1, keepdims=True) + 1e-05)
            hidden = (x * rinv * g_ref[loop]).astype(BF16)
            for place in range(across):
                for half in range(FAR):
                    at = (half * across + place) * near
                    tiles_ref[
                        lax.rem(place + across - where[1], across),
                        loop,
                        rows,
                        half * near : (half + 1) * near,
                    ] = hidden[:, at : at + near]
        return carry

    lax.fori_loop(0, tok // ROWS, one, 0)


def rows_kernel(where, mine_ref, other_ref, w_ref):
    count, piece, _ = mine_ref.shape
    for index in range(count):
        for ref, core in ((mine_ref, where[2]), (other_ref, 1 - where[2])):
            at = pl.multiple_of((2 * index + core) * piece, piece)
            w_ref[pl.ds(at, piece), :] = ref[index]


def part_kernel(*refs):
    part_ref = refs[-1]
    count = (len(refs) - 1) // 2
    total = None
    for tiles_ref, dv_ref in zip(refs[:count], refs[count:-1], strict=True):
        tok = tiles_ref.shape[1]
        for loop in range(2):
            at = 0 if loop == 0 else tok
            term = lax.dot_general(
                tiles_ref[loop],
                dv_ref[at : at + tok, :],
                (((0,), (0,)), ((), ())),
                preferred_element_type=F32,
            )
            total = term if total is None else total + term
    part_ref[...] = total.astype(BF16)


def task_of(step, section, npipe):
    return step - SLACK * (npipe - 1 - section)


def step_kernel(step, npipe, blocks, where, w_ref, x_ref, g_ref, fresh_ref, in_ref, *refs):
    dx_ref, dv_ref = refs[-2:]
    section = where[0]
    task = task_of(step, section, npipe)

    @pl.when((task >= 0) & (task < 2 * blocks))
    def _():
        later = task < blocks
        loop = jnp.where(later, 1, 0)
        block = jnp.where(later, task, task - blocks)
        row = pl.multiple_of(block * ROWS, ROWS)
        width = dx_ref.shape[1]
        kv_width = dv_ref.shape[1]
        heads = kv_width // HEAD
        group = width // kv_width
        take = later & (section == npipe - 1)
        dy = jnp.where(take, fresh_ref[pl.ds(row, ROWS), :], in_ref[...]).astype(F32)
        x = x_ref[loop, pl.ds(row, ROWS), :].astype(F32)
        sums = []
        for head in range(heads):
            base = head * group * HEAD
            total = dy[:, base : base + HEAD]
            for member in range(1, group):
                at = base + member * HEAD
                total = total + dy[:, at : at + HEAD]
            sums.append(total)
        dv = jnp.concatenate(sums, axis=1).astype(BF16)
        dv_ref[...] = dv
        dh = lax.dot_general(
            dv, w_ref[...], (((1,), (1,)), ((), ())), preferred_element_type=F32
        )
        dhg = dh * g_ref[loop]
        rinv = lax.rsqrt(jnp.mean(x * x, axis=-1, keepdims=True) + 1e-05)
        normed = x * rinv
        along = jnp.mean(dhg * normed, axis=-1, keepdims=True)
        dx_ref[...] = (dy + rinv * (dhg - normed * along)).astype(BF16)


def collect_kernel(npipe, blocks, where, *refs):
    *pieces, out_ref, sems = refs
    section = where[0]

    def each(act):
        for step, piece in enumerate(pieces):
            task = task_of(step, section, npipe)

            @pl.when((task >= 0) & (task < 2 * blocks))
            def _():
                later = task < blocks
                loop = jnp.where(later, 1, 0)
                row = pl.multiple_of((task - jnp.where(later, 0, blocks)) * ROWS, ROWS)
                target = out_ref.at[loop, pl.ds(row, ROWS), :]
                act(pltpu.make_async_copy(piece, target, sems.at[step]))

    each(lambda copy: copy.start())
    each(lambda copy: copy.wait())


def stack_kernel(npipe, blocks, where, *refs):
    *pieces, out_ref = refs
    section = where[0]
    for step, piece in enumerate(pieces):
        task = task_of(step, section, npipe)

        @pl.when((task >= 0) & (task < 2 * blocks))
        def _():
            place = task + jnp.where(task < blocks, blocks, -blocks)
            out_ref[pl.ds(pl.multiple_of(place * ROWS, ROWS), ROWS), :] = piece[...]


def exchanged(pieces, axis):
    count = lax.axis_size(axis)
    moved = [pieces[0]]
    for shift in range(1, count):
        pairs = [(source, (source + shift) % count) for source in range(count)]
        moved.append(lax.ppermute(pieces[shift], axis, pairs))
    return moved


def on_device(saved, grad_out, gain, w_value):
    npipe = lax.axis_size("pipe")
    where = jnp.stack([lax.axis_index(name) for name in ("pipe", "dp_1", "dp_3")]).astype(jnp.int32)
    x = saved[:, 0]
    _, tok, width = x.shape
    kv_width = w_value.shape[2]
    blocks = tok // ROWS
    across = lax.axis_size("dp_1")
    shape = jax.ShapeDtypeStruct

    mine = copy_for_each(w_value[0], DP[:3])
    other = lax.ppermute(mine, DP[3], [(0, 1), (1, 0)])
    w_mat = kernel_call(
        rows_kernel,
        "rows",
        shape((width, kv_width), BF16),
        [IN_SMEM] + [IN_VMEM] * 2,
        (where, mine, other),
    )

    steps = 2 * blocks + SLACK * (npipe - 1)
    sent, gx_parts, gv_parts = {}, [], []
    for step in range(steps):
        incoming = sent.pop(step - SLACK, None)
        if incoming is None:
            incoming = jnp.zeros((ROWS, width), BF16)
        later = tuple(hidden[1:]) if step == HIDDEN_BY else ()
        turn = gv_parts[-1:]
        if step in (1, 3, 5):
            turn = [*turn, sent[step - 1]]
        dx, dv = kernel_call(
            functools.partial(step_kernel, step, npipe, blocks),
            "section_step",
            (shape((ROWS, width), BF16), shape((ROWS, kv_width), BF16)),
            [IN_SMEM] + [IN_VMEM] * (5 + len(turn)) + [ANYWHERE] * len(later),
            (where, w_mat, x, gain, grad_out, incoming, *turn, *later),
        )
        gx_parts.append(dx)
        gv_parts.append(dv)
        pairs = []
        for source in range(npipe):
            task = task_of(step, source, npipe)
            if 0 <= task < (blocks if source == 0 else 2 * blocks):
                pairs.append((source, (source - 1) % npipe))
        if pairs:
            sent[step] = lax.ppermute(dx, "pipe", pairs)
        if step == HIDDEN_AT:
            tiles = kernel_call(
                norm_kernel,
                "normalize",
                shape((across, 2, tok, width // across), BF16),
                [IN_SMEM] + [IN_VMEM] * 3,
                (where, x, gain, dv),
            )
            hidden = exchanged(tiles, "dp_1")

    grad_x = kernel_call(
        functools.partial(collect_kernel, npipe, blocks),
        "collect_rows",
        shape((2, tok, width), BF16),
        [IN_SMEM] + [IN_VMEM] * steps,
        (where, *gx_parts),
        scratch=(pltpu.SemaphoreType.DMA((steps,)),),
        out_spec=ANYWHERE,
    )[:, None]
    dv_all = kernel_call(
        functools.partial(stack_kernel, npipe, blocks),
        "stack",
        shape((2 * tok, kv_width), BF16),
        [IN_SMEM] + [IN_VMEM] * steps,
        (where, *gv_parts),
    )
    spread = exchanged([dv_all] * across, "dp_1")
    part = kernel_call(
        part_kernel,
        "part",
        shape((width // across, kv_width), BF16),
        [IN_VMEM] * (2 * across),
        (*hidden, *spread),
    )
    others = ("dp_0", "dp_2", "dp_3")
    pieces = part.reshape(lax.axis_size(others), -1, kv_width)
    landed = lax.all_to_all(pieces, others, 0, 0, tiled=True)
    grad_w = landed.astype(F32).sum(axis=0)[None]
    return (grad_x, grad_w)


def solution(mesh):
    finer = Mesh(
        mesh.devices.reshape(mesh.shape["pipe"], 2, 4, 4, 2),
        ("pipe", "dp_0", "dp_1", "dp_2", "dp_3"),
    )
    placed = (P(None, "pipe", DP, None), P(DP, None), P(None, "pipe", None), P("pipe", DP, None))
    return jax.shard_map(
        on_device,
        mesh=finer,
        in_specs=placed,
        out_specs=(P(None, "pipe", DP, None), P("pipe", DP, None)),
        check_vma=False,
    )
```

```python
import functools

import jax
import jax.numpy as jnp
from jax import lax
from jax.experimental import pallas as pl
from jax.experimental.pallas import tpu as pltpu
from jax.sharding import Mesh
from jax.sharding import PartitionSpec as P

HEAD = 128
ROWS = 16
SLACK = 2
FAR = 2
HIDDEN_BY = 6
EARLY = 8
EARLY_BY = 18
DP = ("dp_0", "dp_1", "dp_2", "dp_3")
IN_VMEM = pl.BlockSpec(memory_space=pltpu.VMEM)
IN_SMEM = pl.BlockSpec(memory_space=pltpu.SMEM)
ANYWHERE = pl.BlockSpec(memory_space=pl.ANY)
BF16, F32 = jnp.bfloat16, jnp.float32


def copy_for_each(array, axis):
    count = lax.axis_size(axis)
    return lax.all_to_all(
        jnp.broadcast_to(array[None], (count, *array.shape)), axis, 0, 0, tiled=True
    )


def kernel_call(kernel, name, out_shape, specs, operands, scratch=(), out_spec=IN_VMEM, room=8):
    return pl.pallas_call(
        kernel,
        out_shape=out_shape,
        in_specs=specs,
        out_specs=jax.tree.map(lambda _: out_spec, out_shape),
        scratch_shapes=list(scratch),
        compiler_params=pltpu.CompilerParams(vmem_limit_bytes=room * 2**20),
        name=name,
    )(*operands)


def held_until(value, token):
    return pl.pallas_call(
        lambda value_ref, token_ref, out_ref: None,
        out_shape=jax.ShapeDtypeStruct(value.shape, value.dtype),
        in_specs=[ANYWHERE, ANYWHERE],
        out_specs=ANYWHERE,
        input_output_aliases={0: 0},
        compiler_params=pltpu.CompilerParams(vmem_limit_bytes=2**20),
        name="held_until",
    )(value, token)


def norm_kernel(where, x_ref, g_ref, *refs):
    *tiles, hidden_ref = refs
    _, tok, width = x_ref.shape
    across = len(tiles)
    near = width // (across * FAR)

    def one(index, carry):
        rows = pl.ds(pl.multiple_of(index * ROWS, ROWS), ROWS)
        for loop in range(2):
            x = x_ref[loop, rows, :].astype(F32)
            rinv = lax.rsqrt(jnp.mean(x * x, axis=-1, keepdims=True) + 1e-05)
            hidden_ref[...] = (x * rinv * g_ref[loop]).astype(BF16)
            for shift, tile_ref in enumerate(tiles):
                place = lax.rem(where[1] + shift, across)
                for half in range(FAR):
                    at = pl.multiple_of((half * across + place) * near, near)
                    tile_ref[loop, rows, half * near : (half + 1) * near] = hidden_ref[
                        :, pl.ds(at, near)
                    ]
        return carry

    lax.fori_loop(0, tok // ROWS, one, 0)


def rows_kernel(where, mine_ref, other_ref, w_ref):
    count, piece, _ = mine_ref.shape
    for index in range(count):
        for ref, core in ((mine_ref, where[2]), (other_ref, 1 - where[2])):
            at = pl.multiple_of((2 * index + core) * piece, piece)
            w_ref[pl.ds(at, piece), :] = ref[index]


def part_kernel(start, across, *refs):
    part_ref = refs[-1]
    total = refs[2 * across][...] if start else None
    for tiles_ref, dv_ref in zip(refs[:across], refs[across : 2 * across], strict=True):
        tok = tiles_ref.shape[1]
        done = 0
        while done < dv_ref.shape[0]:
            loop, row = 1 - (start + done) // tok, (start + done) % tok
            count = min(tok - row, dv_ref.shape[0] - done)
            term = lax.dot_general(
                tiles_ref[loop, row : row + count, :],
                dv_ref[done : done + count, :],
                (((0,), (0,)), ((), ())),
                preferred_element_type=F32,
            )
            total = term if total is None else total + term
            done += count
    part_ref[...] = total.astype(part_ref.dtype)


def task_of(step, section, npipe):
    return step - SLACK * (npipe - 1 - section)


def step_kernel(step, npipe, blocks, where, w_ref, x_ref, g_ref, fresh_ref, in_ref, *refs):
    dx_ref, dv_ref = refs[-2:]
    section = where[0]
    task = task_of(step, section, npipe)

    @pl.when((task >= 0) & (task < 2 * blocks))
    def _():
        later = task < blocks
        loop = jnp.where(later, 1, 0)
        block = jnp.where(later, task, task - blocks)
        row = pl.multiple_of(block * ROWS, ROWS)
        width = dx_ref.shape[1]
        kv_width = dv_ref.shape[1]
        heads = kv_width // HEAD
        group = width // kv_width
        take = later & (section == npipe - 1)
        dy = jnp.where(take, fresh_ref[pl.ds(row, ROWS), :], in_ref[...]).astype(F32)
        x = x_ref[loop, pl.ds(row, ROWS), :].astype(F32)
        sums = []
        for head in range(heads):
            base = head * group * HEAD
            total = dy[:, base : base + HEAD]
            for member in range(1, group):
                at = base + member * HEAD
                total = total + dy[:, at : at + HEAD]
            sums.append(total)
        dv = jnp.concatenate(sums, axis=1).astype(BF16)
        dv_ref[...] = dv
        dh = lax.dot_general(
            dv, w_ref[...], (((1,), (1,)), ((), ())), preferred_element_type=F32
        )
        dhg = dh * g_ref[loop]
        rinv = lax.rsqrt(jnp.mean(x * x, axis=-1, keepdims=True) + 1e-05)
        normed = x * rinv
        along = jnp.mean(dhg * normed, axis=-1, keepdims=True)
        dx_ref[...] = (dy + rinv * (dhg - normed * along)).astype(BF16)


def collect_kernel(npipe, blocks, where, *refs):
    *pieces, out_ref, sems = refs
    section = where[0]

    def each(act):
        for step, piece in enumerate(pieces):
            task = task_of(step, section, npipe)

            @pl.when((task >= 0) & (task < 2 * blocks))
            def _():
                later = task < blocks
                loop = jnp.where(later, 1, 0)
                row = pl.multiple_of((task - jnp.where(later, 0, blocks)) * ROWS, ROWS)
                target = out_ref.at[loop, pl.ds(row, ROWS), :]
                act(pltpu.make_async_copy(piece, target, sems.at[step]))

    each(lambda copy: copy.start())
    each(lambda copy: copy.wait())


def stack_kernel(npipe, start, where, *refs):
    *pieces, out_ref = refs
    section = where[0]
    count = out_ref.shape[0] // ROWS
    for step, piece in enumerate(pieces):
        place = task_of(step, section, npipe) - start

        @pl.when((place >= 0) & (place < count))
        def _():
            out_ref[pl.ds(pl.multiple_of(place * ROWS, ROWS), ROWS), :] = piece[...]


def exchanged(pieces, axis):
    count = lax.axis_size(axis)
    moved = [pieces[0]]
    for shift in range(1, count):
        pairs = [(source, (source + shift) % count) for source in range(count)]
        moved.append(lax.ppermute(pieces[shift], axis, pairs))
    return moved


def on_device(saved, grad_out, gain, w_value):
    npipe = lax.axis_size("pipe")
    where = jnp.stack([lax.axis_index(name) for name in ("pipe", "dp_1", "dp_3")]).astype(jnp.int32)
    stage = lax.axis_index("pipe").astype(jnp.int32).reshape(1)
    x = saved[:, 0]
    _, tok, width = x.shape
    kv_width = w_value.shape[2]
    blocks = tok // ROWS
    across = lax.axis_size("dp_1")
    shape = jax.ShapeDtypeStruct

    tiles = kernel_call(
        norm_kernel,
        "normalize",
        (shape((2, tok, width // across), BF16),) * across,
        [IN_SMEM] + [IN_VMEM] * 2,
        (where, x, gain),
        scratch=(pltpu.VMEM((ROWS, width), BF16),),
    )
    mine = held_until(copy_for_each(w_value[0], DP[:3]), tiles[0])
    other = lax.ppermute(mine, DP[3], [(0, 1), (1, 0)])
    hidden = exchanged(tiles, "dp_1")
    w_mat = kernel_call(
        rows_kernel,
        "rows",
        shape((width, kv_width), BF16),
        [IN_SMEM] + [IN_VMEM] * 2,
        (where, mine, other),
    )

    def partial_sum(start, end, extra, kind):
        rows = (end - start) * ROWS
        dv = kernel_call(
            functools.partial(stack_kernel, npipe, start),
            "stack",
            shape((rows, kv_width), BF16),
            [IN_SMEM] + [IN_VMEM] * len(gv_parts),
            (stage, *gv_parts),
        )
        spread = exchanged([dv] * across, "dp_1")
        return kernel_call(
            functools.partial(part_kernel, start * ROWS, across),
            "part",
            shape((width // across, kv_width), kind),
            [IN_VMEM] * (2 * across + len(extra)),
            (*hidden, *spread, *extra),
        )

    steps = 2 * blocks + SLACK * (npipe - 1)
    sent, gx_parts, gv_parts = {}, [], []
    for step in range(steps):
        incoming = sent.pop(step - SLACK, None)
        if incoming is None:
            incoming = jnp.zeros((ROWS, width), BF16)
        later = ()
        if step == HIDDEN_BY:
            later = tuple(hidden[1:])
        elif step == EARLY_BY:
            later = (early,)
        turn = gv_parts[-1:]
        dx, dv = kernel_call(
            functools.partial(step_kernel, step, npipe, blocks),
            "section_step",
            (shape((ROWS, width), BF16), shape((ROWS, kv_width), BF16)),
            [IN_SMEM] + [IN_VMEM] * (5 + len(turn)) + [ANYWHERE] * len(later),
            (stage, w_mat, x, gain, grad_out, incoming, *turn, *later),
        )
        gx_parts.append(dx)
        gv_parts.append(dv)
        pairs = []
        for source in range(npipe):
            task = task_of(step, source, npipe)
            if 0 <= task < (blocks if source == 0 else 2 * blocks):
                pairs.append((source, (source - 1) % npipe))
        if pairs:
            sent[step] = lax.ppermute(dx, "pipe", pairs)
        if step == EARLY + SLACK * (npipe - 1) - 1:
            early = partial_sum(0, EARLY, (), F32)

    grad_x = kernel_call(
        functools.partial(collect_kernel, npipe, blocks),
        "collect_rows",
        shape((2, tok, width), BF16),
        [IN_SMEM] + [IN_VMEM] * steps,
        (stage, *gx_parts),
        scratch=(pltpu.SemaphoreType.DMA((steps,)),),
        out_spec=ANYWHERE,
    )[:, None]
    part = partial_sum(EARLY, 2 * blocks, (early,), BF16)
    others = ("dp_0", "dp_2", "dp_3")
    pieces = part.reshape(lax.axis_size(others), -1, kv_width)
    landed = lax.all_to_all(pieces, others, 0, 0, tiled=True)
    grad_w = landed.astype(F32).sum(axis=0)[None]
    return (grad_x, grad_w)


def solution(mesh):
    finer = Mesh(
        mesh.devices.reshape(mesh.shape["pipe"], 2, 4, 4, 2),
        ("pipe", "dp_0", "dp_1", "dp_2", "dp_3"),
    )
    placed = (P(None, "pipe", DP, None), P(DP, None), P(None, "pipe", None), P("pipe", DP, None))
    return jax.shard_map(
        on_device,
        mesh=finer,
        in_specs=placed,
        out_specs=(P(None, "pipe", DP, None), P("pipe", DP, None)),
        check_vma=False,
    )
```

```python
import functools

import jax
import jax.numpy as jnp
from jax import lax
from jax.experimental import pallas as pl
from jax.experimental.pallas import tpu as pltpu
from jax.sharding import Mesh
from jax.sharding import PartitionSpec as P

HEAD = 128
ROWS = 16
SLACK = 2
FAR = 2
HIDDEN_BY = 6
EARLY = 8
EARLY_BY = 18
DP = ("dp_0", "dp_1", "dp_2", "dp_3")
IN_VMEM = pl.BlockSpec(memory_space=pltpu.VMEM)
IN_SMEM = pl.BlockSpec(memory_space=pltpu.SMEM)
ANYWHERE = pl.BlockSpec(memory_space=pl.ANY)
BF16, F32 = jnp.bfloat16, jnp.float32


def copy_for_each(array, axis):
    count = lax.axis_size(axis)
    return lax.all_to_all(
        jnp.broadcast_to(array[None], (count, *array.shape)), axis, 0, 0, tiled=True
    )


def kernel_call(kernel, name, out_shape, specs, operands, scratch=(), out_spec=IN_VMEM, room=8):
    return pl.pallas_call(
        kernel,
        out_shape=out_shape,
        in_specs=specs,
        out_specs=jax.tree.map(lambda _: out_spec, out_shape),
        scratch_shapes=list(scratch),
        compiler_params=pltpu.CompilerParams(vmem_limit_bytes=room * 2**20),
        name=name,
    )(*operands)


def held_until(value, token):
    return pl.pallas_call(
        lambda value_ref, token_ref, out_ref: None,
        out_shape=jax.ShapeDtypeStruct(value.shape, value.dtype),
        in_specs=[ANYWHERE, ANYWHERE],
        out_specs=ANYWHERE,
        input_output_aliases={0: 0},
        compiler_params=pltpu.CompilerParams(vmem_limit_bytes=2**20),
        name="held_until",
    )(value, token)


def norm_kernel(where, x_ref, g_ref, *refs):
    *tiles, hidden_ref = refs
    _, tok, width = x_ref.shape
    across = len(tiles)
    near = width // (across * FAR)

    def one(index, carry):
        rows = pl.ds(pl.multiple_of(index * ROWS, ROWS), ROWS)
        for loop in range(2):
            x = x_ref[loop, rows, :].astype(F32)
            rinv = lax.rsqrt(jnp.mean(x * x, axis=-1, keepdims=True) + 1e-05)
            hidden_ref[...] = (x * rinv * g_ref[loop]).astype(BF16)
            for shift, tile_ref in enumerate(tiles):
                place = lax.rem(where[1] + shift, across)
                for half in range(FAR):
                    at = pl.multiple_of((half * across + place) * near, near)
                    tile_ref[loop, rows, half * near : (half + 1) * near] = hidden_ref[
                        :, pl.ds(at, near)
                    ]
        return carry

    lax.fori_loop(0, tok // ROWS, one, 0)


def rows_kernel(where, mine_ref, other_ref, w_ref):
    count, piece, _ = mine_ref.shape
    for index in range(count):
        for ref, core in ((mine_ref, where[2]), (other_ref, 1 - where[2])):
            at = pl.multiple_of((2 * index + core) * piece, piece)
            w_ref[pl.ds(at, piece), :] = ref[index]


def part_kernel(start, across, where, *refs):
    total = refs[2 * across][...] if start else None
    for tiles_ref, dv_ref in zip(refs[:across], refs[across : 2 * across], strict=True):
        tok = tiles_ref.shape[1]
        done = 0
        while done < dv_ref.shape[0]:
            loop, row = 1 - (start + done) // tok, (start + done) % tok
            count = min(tok - row, dv_ref.shape[0] - done)
            term = lax.dot_general(
                tiles_ref[loop, row : row + count, :],
                dv_ref[done : done + count, :],
                (((0,), (0,)), ((), ())),
                preferred_element_type=F32,
            )
            total = term if total is None else total + term
            done += count
    if not start:
        refs[-1][...] = total
        return
    keep_ref, give_ref, total_ref = refs[-3:]
    total_ref[...] = total
    count, piece, _ = keep_ref.shape
    for index in range(count):
        at = pl.multiple_of((2 * index + where[2]) * piece, piece)
        keep_ref[index] = total_ref[pl.ds(at, piece), :]
        at = pl.multiple_of((2 * index + 1 - where[2]) * piece, piece)
        give_ref[index] = total_ref[pl.ds(at, piece), :].astype(BF16)


def pair_kernel(keep_ref, got_ref, out_ref):
    out_ref[...] = (keep_ref[...] + got_ref[...].astype(F32)).astype(BF16)


def sum_kernel(pieces_ref, out_ref):
    total = pieces_ref[0].astype(F32)
    for index in range(1, pieces_ref.shape[0]):
        total = total + pieces_ref[index].astype(F32)
    out_ref[...] = total


def task_of(step, section, npipe):
    return step - SLACK * (npipe - 1 - section)


def step_kernel(step, npipe, blocks, where, w_ref, x_ref, g_ref, fresh_ref, in_ref, *refs):
    dx_ref, dv_ref = refs[-2:]
    section = where[0]
    task = task_of(step, section, npipe)

    @pl.when((task >= 0) & (task < 2 * blocks))
    def _():
        later = task < blocks
        loop = jnp.where(later, 1, 0)
        block = jnp.where(later, task, task - blocks)
        row = pl.multiple_of(block * ROWS, ROWS)
        width = dx_ref.shape[1]
        kv_width = dv_ref.shape[1]
        heads = kv_width // HEAD
        group = width // kv_width
        take = later & (section == npipe - 1)
        dy = jnp.where(take, fresh_ref[pl.ds(row, ROWS), :], in_ref[...]).astype(F32)
        x = x_ref[loop, pl.ds(row, ROWS), :].astype(F32)
        sums = []
        for head in range(heads):
            base = head * group * HEAD
            total = dy[:, base : base + HEAD]
            for member in range(1, group):
                at = base + member * HEAD
                total = total + dy[:, at : at + HEAD]
            sums.append(total)
        dv = jnp.concatenate(sums, axis=1).astype(BF16)
        dv_ref[...] = dv
        dh = lax.dot_general(
            dv, w_ref[...], (((1,), (1,)), ((), ())), preferred_element_type=F32
        )
        dhg = dh * g_ref[loop]
        rinv = lax.rsqrt(jnp.mean(x * x, axis=-1, keepdims=True) + 1e-05)
        normed = x * rinv
        along = jnp.mean(dhg * normed, axis=-1, keepdims=True)
        dx_ref[...] = (dy + rinv * (dhg - normed * along)).astype(BF16)


def collect_kernel(npipe, blocks, where, *refs):
    *pieces, out_ref, sems = refs
    section = where[0]

    def each(act):
        for step, piece in enumerate(pieces):
            task = task_of(step, section, npipe)

            @pl.when((task >= 0) & (task < 2 * blocks))
            def _():
                later = task < blocks
                loop = jnp.where(later, 1, 0)
                row = pl.multiple_of((task - jnp.where(later, 0, blocks)) * ROWS, ROWS)
                target = out_ref.at[loop, pl.ds(row, ROWS), :]
                act(pltpu.make_async_copy(piece, target, sems.at[step]))

    each(lambda copy: copy.start())
    each(lambda copy: copy.wait())


def stack_kernel(npipe, start, where, *refs):
    *pieces, out_ref = refs
    section = where[0]
    count = out_ref.shape[0] // ROWS
    for step, piece in enumerate(pieces):
        place = task_of(step, section, npipe) - start

        @pl.when((place >= 0) & (place < count))
        def _():
            out_ref[pl.ds(pl.multiple_of(place * ROWS, ROWS), ROWS), :] = piece[...]


def exchanged(pieces, axis):
    count = lax.axis_size(axis)
    moved = [pieces[0]]
    for shift in range(1, count):
        pairs = [(source, (source + shift) % count) for source in range(count)]
        moved.append(lax.ppermute(pieces[shift], axis, pairs))
    return moved


def on_device(saved, grad_out, gain, w_value):
    npipe = lax.axis_size("pipe")
    where = jnp.stack([lax.axis_index(name) for name in ("pipe", "dp_1", "dp_3")]).astype(jnp.int32)
    stage = lax.axis_index("pipe").astype(jnp.int32).reshape(1)
    x = saved[:, 0]
    _, tok, width = x.shape
    kv_width = w_value.shape[2]
    blocks = tok // ROWS
    across = lax.axis_size("dp_1")
    shape = jax.ShapeDtypeStruct

    tiles = kernel_call(
        norm_kernel,
        "normalize",
        (shape((2, tok, width // across), BF16),) * across,
        [IN_SMEM] + [IN_VMEM] * 2,
        (where, x, gain),
        scratch=(pltpu.VMEM((ROWS, width), BF16),),
    )
    mine = held_until(copy_for_each(w_value[0], DP[:3]), tiles[0])
    other = lax.ppermute(mine, DP[3], [(0, 1), (1, 0)])
    hidden = exchanged(tiles, "dp_1")
    w_mat = kernel_call(
        rows_kernel,
        "rows",
        shape((width, kv_width), BF16),
        [IN_SMEM] + [IN_VMEM] * 2,
        (where, mine, other),
    )

    def partial_sum(start, end, extra):
        rows, whole = (end - start) * ROWS, width // across
        dv = kernel_call(
            functools.partial(stack_kernel, npipe, start),
            "stack",
            shape((rows, kv_width), BF16),
            [IN_SMEM] + [IN_VMEM] * len(gv_parts),
            (stage, *gv_parts),
        )
        spread = exchanged([dv] * across, "dp_1")
        kinds = (shape(halves, F32), shape(halves, BF16)) if start else shape((whole, kv_width), F32)
        return kernel_call(
            functools.partial(part_kernel, start * ROWS, across),
            "part",
            kinds,
            [IN_SMEM] + [IN_VMEM] * (2 * across + len(extra)),
            (where, *hidden, *spread, *extra),
            scratch=(pltpu.VMEM((whole, kv_width), F32),) if start else (),
        )

    others = ("dp_0", "dp_2")
    count = lax.axis_size(others)
    halves = (count, w_value.shape[1], kv_width)
    steps = 2 * blocks + SLACK * (npipe - 1)
    sent, gx_parts, gv_parts = {}, [], []
    for step in range(steps):
        incoming = sent.pop(step - SLACK, None)
        if incoming is None:
            incoming = jnp.zeros((ROWS, width), BF16)
        later = ()
        if step == HIDDEN_BY:
            later = tuple(hidden[1:])
        elif step == EARLY_BY:
            later = (early,)
        turn = gv_parts[-1:]
        dx, dv = kernel_call(
            functools.partial(step_kernel, step, npipe, blocks),
            "section_step",
            (shape((ROWS, width), BF16), shape((ROWS, kv_width), BF16)),
            [IN_SMEM] + [IN_VMEM] * (5 + len(turn)) + [ANYWHERE] * len(later),
            (stage, w_mat, x, gain, grad_out, incoming, *turn, *later),
        )
        gx_parts.append(dx)
        gv_parts.append(dv)
        pairs = []
        for source in range(npipe):
            task = task_of(step, source, npipe)
            if 0 <= task < (blocks if source == 0 else 2 * blocks):
                pairs.append((source, (source - 1) % npipe))
        if pairs:
            sent[step] = lax.ppermute(dx, "pipe", pairs)
        if step == EARLY + SLACK * (npipe - 1) - 1:
            early = partial_sum(0, EARLY, ())

    grad_x = kernel_call(
        functools.partial(collect_kernel, npipe, blocks),
        "collect_rows",
        shape((2, tok, width), BF16),
        [IN_SMEM] + [IN_VMEM] * steps,
        (stage, *gx_parts),
        scratch=(pltpu.SemaphoreType.DMA((steps,)),),
        out_spec=ANYWHERE,
    )[:, None]
    keep, give = partial_sum(EARLY, 2 * blocks, (early,))
    got = lax.ppermute(give, DP[3], [(0, 1), (1, 0)])
    paired = kernel_call(pair_kernel, "pair", shape(halves, BF16), [IN_VMEM] * 2, (keep, got))
    landed = lax.all_to_all(paired, others, 0, 0, tiled=True)
    grad_w = kernel_call(sum_kernel, "sum", shape(halves[1:], F32), [IN_VMEM], (landed,))[None]
    return (grad_x, grad_w)


def solution(mesh):
    finer = Mesh(
        mesh.devices.reshape(mesh.shape["pipe"], 2, 4, 4, 2),
        ("pipe", "dp_0", "dp_1", "dp_2", "dp_3"),
    )
    placed = (P(None, "pipe", DP, None), P(DP, None), P(None, "pipe", None), P("pipe", DP, None))
    return jax.shard_map(
        on_device,
        mesh=finer,
        in_specs=placed,
        out_specs=(P(None, "pipe", DP, None), P("pipe", DP, None)),
        check_vma=False,
    )
```

```python
import functools

import jax
import jax.numpy as jnp
from jax import lax
from jax.experimental import pallas as pl
from jax.experimental.pallas import tpu as pltpu
from jax.sharding import Mesh
from jax.sharding import PartitionSpec as P

HEAD = 128
ROWS = 16
SLACK = 2
FAR = 2
HIDDEN_BY = 6
EARLY = 8
EARLY_BY = 18
DP = ("dp_0", "dp_1", "dp_2", "dp_3")
IN_VMEM = pl.BlockSpec(memory_space=pltpu.VMEM)
IN_SMEM = pl.BlockSpec(memory_space=pltpu.SMEM)
ANYWHERE = pl.BlockSpec(memory_space=pl.ANY)
BF16, F32 = jnp.bfloat16, jnp.float32


def copy_for_each(array, axis):
    count = lax.axis_size(axis)
    return lax.all_to_all(
        jnp.broadcast_to(array[None], (count, *array.shape)), axis, 0, 0, tiled=True
    )


def kernel_call(kernel, name, out_shape, specs, operands, scratch=(), out_spec=IN_VMEM, room=8):
    return pl.pallas_call(
        kernel,
        out_shape=out_shape,
        in_specs=specs,
        out_specs=jax.tree.map(lambda _: out_spec, out_shape),
        scratch_shapes=list(scratch),
        compiler_params=pltpu.CompilerParams(vmem_limit_bytes=room * 2**20),
        name=name,
    )(*operands)


def held_until(value, token):
    return pl.pallas_call(
        lambda value_ref, token_ref, out_ref: None,
        out_shape=jax.ShapeDtypeStruct(value.shape, value.dtype),
        in_specs=[ANYWHERE, ANYWHERE],
        out_specs=ANYWHERE,
        input_output_aliases={0: 0},
        compiler_params=pltpu.CompilerParams(vmem_limit_bytes=2**20),
        name="held_until",
    )(value, token)


def norm_kernel(where, x_ref, g_ref, *refs):
    *tiles, hidden_ref = refs
    _, tok, width = x_ref.shape
    across = len(tiles)
    near = width // (across * FAR)

    def one(index, carry):
        rows = pl.ds(pl.multiple_of(index * ROWS, ROWS), ROWS)
        for loop in range(2):
            x = x_ref[loop, rows, :].astype(F32)
            rinv = lax.rsqrt(jnp.mean(x * x, axis=-1, keepdims=True) + 1e-05)
            hidden_ref[...] = (x * rinv * g_ref[loop]).astype(BF16)
            for shift, tile_ref in enumerate(tiles):
                place = lax.rem(where[1] + shift, across)
                for half in range(FAR):
                    at = pl.multiple_of((half * across + place) * near, near)
                    tile_ref[loop, rows, half * near : (half + 1) * near] = hidden_ref[
                        :, pl.ds(at, near)
                    ]
        return carry

    lax.fori_loop(0, tok // ROWS, one, 0)


def rows_kernel(where, *refs):
    *sets, w_ref = refs
    wide, piece = sets[0].shape[1], sets[0].shape[0] // 32
    for index, ref in enumerate(sets):
        half, other = index % 2, index // 2
        core = (1 - where[2]) if other else where[2]
        for order in range(32):
            outer, inner, depth = order // 8, order // 2 % 4, order % 2
            over_x, over_y = (inner, outer) if half == 0 else (outer, inner)
            z = lax.rem(where[3] + depth, 2)
            x = lax.rem(where[1] + 4 - over_x, 4)
            y = lax.rem(where[4] + 4 - over_y, 4)
            at = pl.multiple_of((((z * 4 + x) * 4 + y) * 2 + core) * piece, piece)
            w_ref[pl.ds(at, piece), half * wide : (half + 1) * wide] = ref[
                order * piece : (order + 1) * piece, :
            ]


def part_kernel(start, across, where, *refs):
    total = refs[2 * across][...] if start else None
    for tiles_ref, dv_ref in zip(refs[:across], refs[across : 2 * across], strict=True):
        tok = tiles_ref.shape[1]
        done = 0
        while done < dv_ref.shape[0]:
            loop, row = 1 - (start + done) // tok, (start + done) % tok
            count = min(tok - row, dv_ref.shape[0] - done)
            term = lax.dot_general(
                tiles_ref[loop, row : row + count, :],
                dv_ref[done : done + count, :],
                (((0,), (0,)), ((), ())),
                preferred_element_type=F32,
            )
            total = term if total is None else total + term
            done += count
    if not start:
        refs[-1][...] = total
        return
    keep_ref, give_ref, total_ref = refs[-3:]
    total_ref[...] = total
    count, piece, _ = keep_ref.shape
    for index in range(count):
        at = pl.multiple_of((2 * index + where[2]) * piece, piece)
        keep_ref[index] = total_ref[pl.ds(at, piece), :]
        at = pl.multiple_of((2 * index + 1 - where[2]) * piece, piece)
        give_ref[index] = total_ref[pl.ds(at, piece), :].astype(BF16)


def pair_kernel(keep_ref, got_ref, out_ref):
    out_ref[...] = (keep_ref[...] + got_ref[...].astype(F32)).astype(BF16)


def sum_kernel(pieces_ref, out_ref):
    total = pieces_ref[0].astype(F32)
    for index in range(1, pieces_ref.shape[0]):
        total = total + pieces_ref[index].astype(F32)
    out_ref[...] = total


def task_of(step, section, npipe):
    return step - SLACK * (npipe - 1 - section)


def step_kernel(step, npipe, blocks, where, w_ref, x_ref, g_ref, fresh_ref, in_ref, *refs):
    dx_ref, dv_ref = refs[-2:]
    section = where[0]
    task = task_of(step, section, npipe)

    @pl.when((task >= 0) & (task < 2 * blocks))
    def _():
        later = task < blocks
        loop = jnp.where(later, 1, 0)
        block = jnp.where(later, task, task - blocks)
        row = pl.multiple_of(block * ROWS, ROWS)
        width = dx_ref.shape[1]
        kv_width = dv_ref.shape[1]
        heads = kv_width // HEAD
        group = width // kv_width
        take = later & (section == npipe - 1)
        dy = jnp.where(take, fresh_ref[pl.ds(row, ROWS), :], in_ref[...]).astype(F32)
        x = x_ref[loop, pl.ds(row, ROWS), :].astype(F32)
        sums = []
        for head in range(heads):
            base = head * group * HEAD
            total = dy[:, base : base + HEAD]
            for member in range(1, group):
                at = base + member * HEAD
                total = total + dy[:, at : at + HEAD]
            sums.append(total)
        dv = jnp.concatenate(sums, axis=1).astype(BF16)
        dv_ref[...] = dv
        dh = lax.dot_general(
            dv, w_ref[...], (((1,), (1,)), ((), ())), preferred_element_type=F32
        )
        dhg = dh * g_ref[loop]
        rinv = lax.rsqrt(jnp.mean(x * x, axis=-1, keepdims=True) + 1e-05)
        normed = x * rinv
        along = jnp.mean(dhg * normed, axis=-1, keepdims=True)
        dx_ref[...] = (dy + rinv * (dhg - normed * along)).astype(BF16)


def collect_kernel(npipe, blocks, where, *refs):
    *pieces, out_ref, sems = refs
    section = where[0]

    def each(act):
        for step, piece in enumerate(pieces):
            task = task_of(step, section, npipe)

            @pl.when((task >= 0) & (task < 2 * blocks))
            def _():
                later = task < blocks
                loop = jnp.where(later, 1, 0)
                row = pl.multiple_of((task - jnp.where(later, 0, blocks)) * ROWS, ROWS)
                target = out_ref.at[loop, pl.ds(row, ROWS), :]
                act(pltpu.make_async_copy(piece, target, sems.at[step]))

    each(lambda copy: copy.start())
    each(lambda copy: copy.wait())


def stack_kernel(npipe, start, where, *refs):
    *pieces, out_ref = refs
    section = where[0]
    count = out_ref.shape[0] // ROWS
    for step, piece in enumerate(pieces):
        place = task_of(step, section, npipe) - start

        @pl.when((place >= 0) & (place < count))
        def _():
            out_ref[pl.ds(pl.multiple_of(place * ROWS, ROWS), ROWS), :] = piece[...]


def exchanged(pieces, axis):
    count = lax.axis_size(axis)
    moved = [pieces[0]]
    for shift in range(1, count):
        pairs = [(source, (source + shift) % count) for source in range(count)]
        moved.append(lax.ppermute(pieces[shift], axis, pairs))
    return moved


def on_device(saved, grad_out, gain, w_value):
    npipe = lax.axis_size("pipe")
    where = jnp.stack([lax.axis_index(name) for name in ("pipe", "dp_1", "dp_3", "dp_0", "dp_2")]).astype(jnp.int32)
    stage = lax.axis_index("pipe").astype(jnp.int32).reshape(1)
    x = saved[:, 0]
    _, tok, width = x.shape
    kv_width = w_value.shape[2]
    blocks = tok // ROWS
    across = lax.axis_size("dp_1")
    shape = jax.ShapeDtypeStruct

    tiles = kernel_call(
        norm_kernel,
        "normalize",
        (shape((2, tok, width // across), BF16),) * across,
        [IN_SMEM] + [IN_VMEM] * 2,
        (where, x, gain),
        scratch=(pltpu.VMEM((ROWS, width), BF16),),
    )
    own = w_value[0]
    pair = jnp.concatenate([own, lax.ppermute(own, DP[0], [(0, 1), (1, 0)])], axis=0)
    middle = kv_width // 2
    sets = []
    for part, axes in ((pair[:, :middle], ("dp_1", "dp_2")), (pair[:, middle:], ("dp_2", "dp_1"))):
        for axis in axes:
            if axis == axes[1] and not sets:
                part = held_until(part, tiles[0])
            part = jnp.concatenate(exchanged([part] * across, axis), axis=0)
        sets.append(part)
    sets += [lax.ppermute(part, DP[3], [(0, 1), (1, 0)]) for part in sets]
    hidden = exchanged(tiles, "dp_1")
    w_mat = kernel_call(
        rows_kernel,
        "rows",
        shape((width, kv_width), BF16),
        [IN_SMEM] + [IN_VMEM] * 4,
        (where, *sets),
    )

    def partial_sum(start, end, extra):
        rows, whole = (end - start) * ROWS, width // across
        dv = kernel_call(
            functools.partial(stack_kernel, npipe, start),
            "stack",
            shape((rows, kv_width), BF16),
            [IN_SMEM] + [IN_VMEM] * len(gv_parts),
            (stage, *gv_parts),
        )
        spread = exchanged([dv] * across, "dp_1")
        kinds = (shape(halves, F32), shape(halves, BF16)) if start else shape((whole, kv_width), F32)
        return kernel_call(
            functools.partial(part_kernel, start * ROWS, across),
            "part",
            kinds,
            [IN_SMEM] + [IN_VMEM] * (2 * across + len(extra)),
            (where, *hidden, *spread, *extra),
            scratch=(pltpu.VMEM((whole, kv_width), F32),) if start else (),
        )

    others = ("dp_0", "dp_2")
    count = lax.axis_size(others)
    halves = (count, w_value.shape[1], kv_width)
    steps = 2 * blocks + SLACK * (npipe - 1)
    sent, gx_parts, gv_parts = {}, [], []
    for step in range(steps):
        incoming = sent.pop(step - SLACK, None)
        if incoming is None:
            incoming = jnp.zeros((ROWS, width), BF16)
        later = ()
        if step == HIDDEN_BY:
            later = tuple(hidden[1:])
        elif step == EARLY_BY:
            later = (early,)
        turn = gv_parts[-1:]
        dx, dv = kernel_call(
            functools.partial(step_kernel, step, npipe, blocks),
            "section_step",
            (shape((ROWS, width), BF16), shape((ROWS, kv_width), BF16)),
            [IN_SMEM] + [IN_VMEM] * (5 + len(turn)) + [ANYWHERE] * len(later),
            (stage, w_mat, x, gain, grad_out, incoming, *turn, *later),
        )
        gx_parts.append(dx)
        gv_parts.append(dv)
        pairs = []
        for source in range(npipe):
            task = task_of(step, source, npipe)
            if 0 <= task < (blocks if source == 0 else 2 * blocks):
                pairs.append((source, (source - 1) % npipe))
        if pairs:
            sent[step] = lax.ppermute(dx, "pipe", pairs)
        if step == EARLY + SLACK * (npipe - 1) - 1:
            early = partial_sum(0, EARLY, ())

    grad_x = kernel_call(
        functools.partial(collect_kernel, npipe, blocks),
        "collect_rows",
        shape((2, tok, width), BF16),
        [IN_SMEM] + [IN_VMEM] * steps,
        (stage, *gx_parts),
        scratch=(pltpu.SemaphoreType.DMA((steps,)),),
        out_spec=ANYWHERE,
    )[:, None]
    keep, give = partial_sum(EARLY, 2 * blocks, (early,))
    got = lax.ppermute(give, DP[3], [(0, 1), (1, 0)])
    paired = kernel_call(pair_kernel, "pair", shape(halves, BF16), [IN_VMEM] * 2, (keep, got))
    landed = lax.all_to_all(paired, others, 0, 0, tiled=True)
    grad_w = kernel_call(sum_kernel, "sum", shape(halves[1:], F32), [IN_VMEM], (landed,))[None]
    return (grad_x, grad_w)


def solution(mesh):
    finer = Mesh(
        mesh.devices.reshape(mesh.shape["pipe"], 2, 4, 4, 2),
        ("pipe", "dp_0", "dp_1", "dp_2", "dp_3"),
    )
    placed = (P(None, "pipe", DP, None), P(DP, None), P(None, "pipe", None), P("pipe", DP, None))
    return jax.shard_map(
        on_device,
        mesh=finer,
        in_specs=placed,
        out_specs=(P(None, "pipe", DP, None), P("pipe", DP, None)),
        check_vma=False,
    )
```

```python
import functools

import jax
import jax.numpy as jnp
from jax import lax
from jax.experimental import pallas as pl
from jax.experimental.pallas import tpu as pltpu
from jax.sharding import Mesh
from jax.sharding import PartitionSpec as P

HEAD = 128
ROWS = 16
SLACK = 2
FAR = 2
HIDDEN_BY = 6
EARLY = 8
EARLY_BY = 19
DP = ("dp_0", "dp_1", "dp_2", "dp_3")
IN_VMEM = pl.BlockSpec(memory_space=pltpu.VMEM)
IN_SMEM = pl.BlockSpec(memory_space=pltpu.SMEM)
ANYWHERE = pl.BlockSpec(memory_space=pl.ANY)
BF16, F32 = jnp.bfloat16, jnp.float32


def copy_for_each(array, axis):
    count = lax.axis_size(axis)
    return lax.all_to_all(
        jnp.broadcast_to(array[None], (count, *array.shape)), axis, 0, 0, tiled=True
    )


def kernel_call(kernel, name, out_shape, specs, operands, scratch=(), out_spec=IN_VMEM, room=8):
    return pl.pallas_call(
        kernel,
        out_shape=out_shape,
        in_specs=specs,
        out_specs=jax.tree.map(lambda _: out_spec, out_shape),
        scratch_shapes=list(scratch),
        compiler_params=pltpu.CompilerParams(vmem_limit_bytes=room * 2**20),
        name=name,
    )(*operands)


def held_until(value, token):
    return pl.pallas_call(
        lambda value_ref, token_ref, out_ref: None,
        out_shape=jax.ShapeDtypeStruct(value.shape, value.dtype),
        in_specs=[ANYWHERE, ANYWHERE],
        out_specs=ANYWHERE,
        input_output_aliases={0: 0},
        compiler_params=pltpu.CompilerParams(vmem_limit_bytes=2**20),
        name="held_until",
    )(value, token)


def norm_kernel(where, x_ref, g_ref, *refs):
    *tiles, hidden_ref = refs
    _, tok, width = x_ref.shape
    across = len(tiles)
    near = width // (across * FAR)

    def one(index, carry):
        rows = pl.ds(pl.multiple_of(index * ROWS, ROWS), ROWS)
        for loop in range(2):
            x = x_ref[loop, rows, :].astype(F32)
            rinv = lax.rsqrt(jnp.mean(x * x, axis=-1, keepdims=True) + 1e-05)
            hidden_ref[...] = (x * rinv * g_ref[loop]).astype(BF16)
            for shift, tile_ref in enumerate(tiles):
                place = lax.rem(where[1] + shift, across)
                for half in range(FAR):
                    at = pl.multiple_of((half * across + place) * near, near)
                    tile_ref[loop, rows, half * near : (half + 1) * near] = hidden_ref[
                        :, pl.ds(at, near)
                    ]
        return carry

    lax.fori_loop(0, tok // ROWS, one, 0)


def rows_kernel(where, mine_ref, other_ref, w_ref):
    count, piece, _ = mine_ref.shape
    for index in range(count):
        for ref, core in ((mine_ref, where[2]), (other_ref, 1 - where[2])):
            at = pl.multiple_of((2 * index + core) * piece, piece)
            w_ref[pl.ds(at, piece), :] = ref[index]


def part_kernel(start, across, where, *refs):
    total = refs[2 * across][...] if start else None
    for tiles_ref, dv_ref in zip(refs[:across], refs[across : 2 * across], strict=True):
        tok = tiles_ref.shape[1]
        done = 0
        while done < dv_ref.shape[0]:
            loop, row = 1 - (start + done) // tok, (start + done) % tok
            count = min(tok - row, dv_ref.shape[0] - done)
            term = lax.dot_general(
                tiles_ref[loop, row : row + count, :],
                dv_ref[done : done + count, :],
                (((0,), (0,)), ((), ())),
                preferred_element_type=F32,
            )
            total = term if total is None else total + term
            done += count
    if not start:
        refs[-1][...] = total
        return
    keep_ref, give_ref, total_ref = refs[-3:]
    total_ref[...] = total
    count, piece, _ = keep_ref.shape
    for index in range(count):
        at = pl.multiple_of((2 * index + where[2]) * piece, piece)
        keep_ref[index] = total_ref[pl.ds(at, piece), :]
        at = pl.multiple_of((2 * index + 1 - where[2]) * piece, piece)
        give_ref[index] = total_ref[pl.ds(at, piece), :].astype(BF16)


def pair_kernel(keep_ref, got_ref, out_ref):
    out_ref[...] = (keep_ref[...] + got_ref[...].astype(F32)).astype(BF16)


def sum_kernel(pieces_ref, out_ref):
    total = pieces_ref[0].astype(F32)
    for index in range(1, pieces_ref.shape[0]):
        total = total + pieces_ref[index].astype(F32)
    out_ref[...] = total


def task_of(step, section, npipe):
    return step - SLACK * (npipe - 1 - section)


def step_kernel(step, npipe, blocks, where, w_ref, x_ref, g_ref, fresh_ref, in_ref, *refs):
    dx_ref, dv_ref = refs[-2:]
    section = where[0]
    task = task_of(step, section, npipe)

    @pl.when((task >= 0) & (task < 2 * blocks))
    def _():
        later = task < blocks
        loop = jnp.where(later, 1, 0)
        block = jnp.where(later, task, task - blocks)
        row = pl.multiple_of(block * ROWS, ROWS)
        width = dx_ref.shape[1]
        kv_width = dv_ref.shape[1]
        heads = kv_width // HEAD
        group = width // kv_width
        take = later & (section == npipe - 1)
        dy = jnp.where(take, fresh_ref[pl.ds(row, ROWS), :], in_ref[...]).astype(F32)
        x = x_ref[loop, pl.ds(row, ROWS), :].astype(F32)
        sums = []
        for head in range(heads):
            base = head * group * HEAD
            total = dy[:, base : base + HEAD]
            for member in range(1, group):
                at = base + member * HEAD
                total = total + dy[:, at : at + HEAD]
            sums.append(total)
        dv = jnp.concatenate(sums, axis=1).astype(BF16)
        dv_ref[...] = dv
        dh = lax.dot_general(
            dv, w_ref[...], (((1,), (1,)), ((), ())), preferred_element_type=F32
        )
        dhg = dh * g_ref[loop]
        rinv = lax.rsqrt(jnp.mean(x * x, axis=-1, keepdims=True) + 1e-05)
        normed = x * rinv
        along = jnp.mean(dhg * normed, axis=-1, keepdims=True)
        dx_ref[...] = (dy + rinv * (dhg - normed * along)).astype(BF16)


def collect_kernel(npipe, blocks, where, *refs):
    *pieces, out_ref, sems = refs
    section = where[0]

    def each(act):
        for step, piece in enumerate(pieces):
            task = task_of(step, section, npipe)

            @pl.when((task >= 0) & (task < 2 * blocks))
            def _():
                later = task < blocks
                loop = jnp.where(later, 1, 0)
                row = pl.multiple_of((task - jnp.where(later, 0, blocks)) * ROWS, ROWS)
                target = out_ref.at[loop, pl.ds(row, ROWS), :]
                act(pltpu.make_async_copy(piece, target, sems.at[step]))

    each(lambda copy: copy.start())
    each(lambda copy: copy.wait())


def stack_kernel(npipe, start, where, *refs):
    *pieces, out_ref = refs
    section = where[0]
    count = out_ref.shape[0] // ROWS
    for step, piece in enumerate(pieces):
        place = task_of(step, section, npipe) - start

        @pl.when((place >= 0) & (place < count))
        def _():
            out_ref[pl.ds(pl.multiple_of(place * ROWS, ROWS), ROWS), :] = piece[...]


def exchanged(pieces, axis):
    count = lax.axis_size(axis)
    moved = [pieces[0]]
    for shift in range(1, count):
        pairs = [(source, (source + shift) % count) for source in range(count)]
        moved.append(lax.ppermute(pieces[shift], axis, pairs))
    return moved


def on_device(saved, grad_out, gain, w_value):
    npipe = lax.axis_size("pipe")
    where = jnp.stack([lax.axis_index(name) for name in ("pipe", "dp_1", "dp_3")]).astype(jnp.int32)
    stage = lax.axis_index("pipe").astype(jnp.int32).reshape(1)
    x = saved[:, 0]
    _, tok, width = x.shape
    kv_width = w_value.shape[2]
    blocks = tok // ROWS
    across = lax.axis_size("dp_1")
    shape = jax.ShapeDtypeStruct

    tiles = kernel_call(
        norm_kernel,
        "normalize",
        (shape((2, tok, width // across), BF16),) * across,
        [IN_SMEM] + [IN_VMEM] * 2,
        (where, x, gain),
        scratch=(pltpu.VMEM((ROWS, width), BF16),),
    )
    mine = held_until(copy_for_each(w_value[0], DP[:3]), tiles[0])
    other = lax.ppermute(mine, DP[3], [(0, 1), (1, 0)])
    hidden = exchanged(tiles, "dp_1")
    w_mat = kernel_call(
        rows_kernel,
        "rows",
        shape((width, kv_width), BF16),
        [IN_SMEM] + [IN_VMEM] * 2,
        (where, mine, other),
    )

    def spread_rows(start, end):
        dv = kernel_call(
            functools.partial(stack_kernel, npipe, start),
            "stack",
            shape(((end - start) * ROWS, kv_width), BF16),
            [IN_SMEM] + [IN_VMEM] * len(gv_parts),
            (stage, *gv_parts),
        )
        return exchanged([dv] * across, "dp_1")

    def partial_sum(start, spread, extra):
        whole = width // across
        kinds = (shape(halves, F32), shape(halves, BF16)) if start else shape((whole, kv_width), F32)
        return kernel_call(
            functools.partial(part_kernel, start * ROWS, across),
            "part",
            kinds,
            [IN_SMEM] + [IN_VMEM] * (2 * across + len(extra)),
            (where, *hidden, *spread, *extra),
            scratch=(pltpu.VMEM((whole, kv_width), F32),) if start else (),
        )

    others = ("dp_0", "dp_2")
    count = lax.axis_size(others)
    halves = (count, w_value.shape[1], kv_width)
    steps = 2 * blocks + SLACK * (npipe - 1)
    sent, gx_parts, gv_parts = {}, [], []
    for step in range(steps):
        incoming = sent.pop(step - SLACK, None)
        if incoming is None:
            incoming = jnp.zeros((ROWS, width), BF16)
        later = ()
        if step == HIDDEN_BY:
            later = tuple(hidden[1:])
        elif step == EARLY_BY:
            later = tuple(early[1:])
        turn = gv_parts[-1:]
        dx, dv = kernel_call(
            functools.partial(step_kernel, step, npipe, blocks),
            "section_step",
            (shape((ROWS, width), BF16), shape((ROWS, kv_width), BF16)),
            [IN_SMEM] + [IN_VMEM] * (5 + len(turn)) + [ANYWHERE] * len(later),
            (stage, w_mat, x, gain, grad_out, incoming, *turn, *later),
        )
        gx_parts.append(dx)
        gv_parts.append(dv)
        pairs = []
        for source in range(npipe):
            task = task_of(step, source, npipe)
            if 0 <= task < (blocks if source == 0 else 2 * blocks):
                pairs.append((source, (source - 1) % npipe))
        if pairs:
            sent[step] = lax.ppermute(dx, "pipe", pairs)
        if step == EARLY + SLACK * (npipe - 1) - 1:
            early = spread_rows(0, EARLY)

    grad_x = kernel_call(
        functools.partial(collect_kernel, npipe, blocks),
        "collect_rows",
        shape((2, tok, width), BF16),
        [IN_SMEM] + [IN_VMEM] * steps,
        (stage, *gx_parts),
        scratch=(pltpu.SemaphoreType.DMA((steps,)),),
        out_spec=ANYWHERE,
    )[:, None]
    late = spread_rows(EARLY, 2 * blocks)
    first = partial_sum(0, early, (late[0],))
    keep, give = partial_sum(EARLY, late, (first,))
    got = lax.ppermute(give, DP[3], [(0, 1), (1, 0)])
    paired = kernel_call(pair_kernel, "pair", shape(halves, BF16), [IN_VMEM] * 2, (keep, got))
    landed = lax.all_to_all(paired, others, 0, 0, tiled=True)
    grad_w = kernel_call(sum_kernel, "sum", shape(halves[1:], F32), [IN_VMEM], (landed,))[None]
    return (grad_x, grad_w)


def solution(mesh):
    finer = Mesh(
        mesh.devices.reshape(mesh.shape["pipe"], 2, 4, 4, 2),
        ("pipe", "dp_0", "dp_1", "dp_2", "dp_3"),
    )
    placed = (P(None, "pipe", DP, None), P(DP, None), P(None, "pipe", None), P("pipe", DP, None))
    return jax.shard_map(
        on_device,
        mesh=finer,
        in_specs=placed,
        out_specs=(P(None, "pipe", DP, None), P("pipe", DP, None)),
        check_vma=False,
    )
```

```python
import functools

import jax
import jax.numpy as jnp
from jax import lax
from jax.experimental import pallas as pl
from jax.experimental.pallas import tpu as pltpu
from jax.sharding import Mesh
from jax.sharding import PartitionSpec as P

HEAD = 128
ROWS = 16
SLACK = 2
FAR = 2
HIDDEN_BY = 6
EARLY = 13
EARLY_BY = 21
DP = ("dp_0", "dp_1", "dp_2", "dp_3")
IN_VMEM = pl.BlockSpec(memory_space=pltpu.VMEM)
IN_SMEM = pl.BlockSpec(memory_space=pltpu.SMEM)
ANYWHERE = pl.BlockSpec(memory_space=pl.ANY)
BF16, F32 = jnp.bfloat16, jnp.float32


def copy_for_each(array, axis):
    count = lax.axis_size(axis)
    return lax.all_to_all(
        jnp.broadcast_to(array[None], (count, *array.shape)), axis, 0, 0, tiled=True
    )


def kernel_call(kernel, name, out_shape, specs, operands, scratch=(), out_spec=IN_VMEM, room=8):
    return pl.pallas_call(
        kernel,
        out_shape=out_shape,
        in_specs=specs,
        out_specs=jax.tree.map(lambda _: out_spec, out_shape),
        scratch_shapes=list(scratch),
        compiler_params=pltpu.CompilerParams(vmem_limit_bytes=room * 2**20),
        name=name,
    )(*operands)


def held_until(value, token):
    return pl.pallas_call(
        lambda value_ref, token_ref, out_ref: None,
        out_shape=jax.ShapeDtypeStruct(value.shape, value.dtype),
        in_specs=[ANYWHERE, ANYWHERE],
        out_specs=ANYWHERE,
        input_output_aliases={0: 0},
        compiler_params=pltpu.CompilerParams(vmem_limit_bytes=2**20),
        name="held_until",
    )(value, token)


def norm_kernel(where, x_ref, g_ref, *refs):
    *tiles, hidden_ref = refs
    _, tok, width = x_ref.shape
    across = len(tiles)
    near = width // (across * FAR)

    def one(index, carry):
        rows = pl.ds(pl.multiple_of(index * ROWS, ROWS), ROWS)
        for loop in range(2):
            x = x_ref[loop, rows, :].astype(F32)
            rinv = lax.rsqrt(jnp.mean(x * x, axis=-1, keepdims=True) + 1e-05)
            hidden_ref[...] = (x * rinv * g_ref[loop]).astype(BF16)
            for shift, tile_ref in enumerate(tiles):
                place = lax.rem(where[1] + shift, across)
                for half in range(FAR):
                    at = pl.multiple_of((half * across + place) * near, near)
                    tile_ref[loop, rows, half * near : (half + 1) * near] = hidden_ref[
                        :, pl.ds(at, near)
                    ]
        return carry

    lax.fori_loop(0, tok // ROWS, one, 0)


def rows_kernel(where, mine_ref, other_ref, w_ref):
    count, piece, _ = mine_ref.shape
    for index in range(count):
        for ref, core in ((mine_ref, where[2]), (other_ref, 1 - where[2])):
            at = pl.multiple_of((2 * index + core) * piece, piece)
            w_ref[pl.ds(at, piece), :] = ref[index]


def part_kernel(start, across, where, *refs):
    total = refs[2 * across][...] if start else None
    for tiles_ref, dv_ref in zip(refs[:across], refs[across : 2 * across], strict=True):
        tok = tiles_ref.shape[1]
        done = 0
        while done < dv_ref.shape[0]:
            loop, row = 1 - (start + done) // tok, (start + done) % tok
            count = min(tok - row, dv_ref.shape[0] - done)
            term = lax.dot_general(
                tiles_ref[loop, row : row + count, :],
                dv_ref[done : done + count, :],
                (((0,), (0,)), ((), ())),
                preferred_element_type=F32,
            )
            total = term if total is None else total + term
            done += count
    if not start:
        refs[-1][...] = total
        return
    keep_ref, give_ref, total_ref = refs[-3:]
    total_ref[...] = total
    count, piece, _ = keep_ref.shape
    for index in range(count):
        at = pl.multiple_of((2 * index + where[2]) * piece, piece)
        keep_ref[index] = total_ref[pl.ds(at, piece), :]
        at = pl.multiple_of((2 * index + 1 - where[2]) * piece, piece)
        give_ref[index] = total_ref[pl.ds(at, piece), :].astype(BF16)


def pair_kernel(keep_ref, got_ref, out_ref):
    out_ref[...] = (keep_ref[...] + got_ref[...].astype(F32)).astype(BF16)


def sum_kernel(pieces_ref, out_ref):
    total = pieces_ref[0].astype(F32)
    for index in range(1, pieces_ref.shape[0]):
        total = total + pieces_ref[index].astype(F32)
    out_ref[...] = total


def task_of(step, section, npipe):
    return step - SLACK * (npipe - 1 - section)


def step_kernel(step, npipe, blocks, where, w_ref, x_ref, g_ref, fresh_ref, in_ref, *refs):
    dx_ref, dv_ref = refs[-2:]
    section = where[0]
    task = task_of(step, section, npipe)

    @pl.when((task >= 0) & (task < 2 * blocks))
    def _():
        later = task < blocks
        loop = jnp.where(later, 1, 0)
        block = jnp.where(later, task, task - blocks)
        row = pl.multiple_of(block * ROWS, ROWS)
        width = dx_ref.shape[1]
        kv_width = dv_ref.shape[1]
        heads = kv_width // HEAD
        group = width // kv_width
        take = later & (section == npipe - 1)
        dy = jnp.where(take, fresh_ref[pl.ds(row, ROWS), :], in_ref[...]).astype(F32)
        x = x_ref[loop, pl.ds(row, ROWS), :].astype(F32)
        sums = []
        for head in range(heads):
            base = head * group * HEAD
            total = dy[:, base : base + HEAD]
            for member in range(1, group):
                at = base + member * HEAD
                total = total + dy[:, at : at + HEAD]
            sums.append(total)
        dv = jnp.concatenate(sums, axis=1).astype(BF16)
        dv_ref[...] = dv
        dh = lax.dot_general(
            dv, w_ref[...], (((1,), (1,)), ((), ())), preferred_element_type=F32
        )
        dhg = dh * g_ref[loop]
        rinv = lax.rsqrt(jnp.mean(x * x, axis=-1, keepdims=True) + 1e-05)
        normed = x * rinv
        along = jnp.mean(dhg * normed, axis=-1, keepdims=True)
        dx_ref[...] = (dy + rinv * (dhg - normed * along)).astype(BF16)


def collect_kernel(npipe, blocks, where, *refs):
    *pieces, out_ref, sems = refs
    section = where[0]

    def each(act):
        for step, piece in enumerate(pieces):
            task = task_of(step, section, npipe)

            @pl.when((task >= 0) & (task < 2 * blocks))
            def _():
                later = task < blocks
                loop = jnp.where(later, 1, 0)
                row = pl.multiple_of((task - jnp.where(later, 0, blocks)) * ROWS, ROWS)
                target = out_ref.at[loop, pl.ds(row, ROWS), :]
                act(pltpu.make_async_copy(piece, target, sems.at[step]))

    each(lambda copy: copy.start())
    each(lambda copy: copy.wait())


def stack_kernel(npipe, start, where, *refs):
    *pieces, out_ref = refs
    section = where[0]
    count = out_ref.shape[0] // ROWS
    for step, piece in enumerate(pieces):
        place = task_of(step, section, npipe) - start

        @pl.when((place >= 0) & (place < count))
        def _():
            out_ref[pl.ds(pl.multiple_of(place * ROWS, ROWS), ROWS), :] = piece[...]


def exchanged(pieces, axis):
    count = lax.axis_size(axis)
    moved = [pieces[0]]
    for shift in range(1, count):
        pairs = [(source, (source + shift) % count) for source in range(count)]
        moved.append(lax.ppermute(pieces[shift], axis, pairs))
    return moved


def on_device(saved, grad_out, gain, w_value):
    npipe = lax.axis_size("pipe")
    where = jnp.stack([lax.axis_index(name) for name in ("pipe", "dp_1", "dp_3")]).astype(jnp.int32)
    stage = lax.axis_index("pipe").astype(jnp.int32).reshape(1)
    x = saved[:, 0]
    _, tok, width = x.shape
    kv_width = w_value.shape[2]
    blocks = tok // ROWS
    across = lax.axis_size("dp_1")
    shape = jax.ShapeDtypeStruct

    tiles = kernel_call(
        norm_kernel,
        "normalize",
        (shape((2, tok, width // across), BF16),) * across,
        [IN_SMEM] + [IN_VMEM] * 2,
        (where, x, gain),
        scratch=(pltpu.VMEM((ROWS, width), BF16),),
    )
    mine = held_until(copy_for_each(w_value[0], DP[:3]), tiles[0])
    other = lax.ppermute(mine, DP[3], [(0, 1), (1, 0)])
    hidden = exchanged(tiles, "dp_1")
    w_mat = kernel_call(
        rows_kernel,
        "rows",
        shape((width, kv_width), BF16),
        [IN_SMEM] + [IN_VMEM] * 2,
        (where, mine, other),
    )

    def spread_rows(start, end):
        dv = kernel_call(
            functools.partial(stack_kernel, npipe, start),
            "stack",
            shape(((end - start) * ROWS, kv_width), BF16),
            [IN_SMEM] + [IN_VMEM] * len(gv_parts),
            (stage, *gv_parts),
        )
        return exchanged([dv] * across, "dp_1")

    def partial_sum(start, spread, extra):
        whole = width // across
        kinds = (shape(halves, F32), shape(halves, BF16)) if start else shape((whole, kv_width), F32)
        return kernel_call(
            functools.partial(part_kernel, start * ROWS, across),
            "part",
            kinds,
            [IN_SMEM] + [IN_VMEM] * (2 * across + len(extra)),
            (where, *hidden, *spread, *extra),
            scratch=(pltpu.VMEM((whole, kv_width), F32),) if start else (),
        )

    others = ("dp_0", "dp_2")
    count = lax.axis_size(others)
    halves = (count, w_value.shape[1], kv_width)
    steps = 2 * blocks + SLACK * (npipe - 1)
    sent, gx_parts, gv_parts = {}, [], []
    for step in range(steps):
        incoming = sent.pop(step - SLACK, None)
        if incoming is None:
            incoming = jnp.zeros((ROWS, width), BF16)
        later = ()
        if step == HIDDEN_BY:
            later = tuple(hidden[1:])
        elif step == EARLY_BY:
            later = tuple(early[1:])
        turn = gv_parts[-1:]
        dx, dv = kernel_call(
            functools.partial(step_kernel, step, npipe, blocks),
            "section_step",
            (shape((ROWS, width), BF16), shape((ROWS, kv_width), BF16)),
            [IN_SMEM] + [IN_VMEM] * (5 + len(turn)) + [ANYWHERE] * len(later),
            (stage, w_mat, x, gain, grad_out, incoming, *turn, *later),
        )
        gx_parts.append(dx)
        gv_parts.append(dv)
        pairs = []
        for source in range(npipe):
            task = task_of(step, source, npipe)
            if 0 <= task < (blocks if source == 0 else 2 * blocks):
                pairs.append((source, (source - 1) % npipe))
        if pairs:
            sent[step] = lax.ppermute(dx, "pipe", pairs)
        if step == EARLY + SLACK * (npipe - 1) - 1:
            early = spread_rows(0, EARLY)

    grad_x = kernel_call(
        functools.partial(collect_kernel, npipe, blocks),
        "collect_rows",
        shape((2, tok, width), BF16),
        [IN_SMEM] + [IN_VMEM] * steps,
        (stage, *gx_parts),
        scratch=(pltpu.SemaphoreType.DMA((steps,)),),
        out_spec=ANYWHERE,
    )[:, None]
    late = spread_rows(EARLY, 2 * blocks)
    first = partial_sum(0, early, (late[0],))
    keep, give = partial_sum(EARLY, late, (first,))
    got = lax.ppermute(give, DP[3], [(0, 1), (1, 0)])
    paired = kernel_call(pair_kernel, "pair", shape(halves, BF16), [IN_VMEM] * 2, (keep, got))
    landed = lax.all_to_all(paired, others, 0, 0, tiled=True)
    grad_w = kernel_call(sum_kernel, "sum", shape(halves[1:], F32), [IN_VMEM], (landed,))[None]
    return (grad_x, grad_w)


def solution(mesh):
    finer = Mesh(
        mesh.devices.reshape(mesh.shape["pipe"], 2, 4, 4, 2),
        ("pipe", "dp_0", "dp_1", "dp_2", "dp_3"),
    )
    placed = (P(None, "pipe", DP, None), P(DP, None), P(None, "pipe", None), P("pipe", DP, None))
    return jax.shard_map(
        on_device,
        mesh=finer,
        in_specs=placed,
        out_specs=(P(None, "pipe", DP, None), P("pipe", DP, None)),
        check_vma=False,
    )
```

```python
import functools

import jax
import jax.numpy as jnp
from jax import lax
from jax.experimental import pallas as pl
from jax.experimental.pallas import tpu as pltpu
from jax.sharding import Mesh
from jax.sharding import PartitionSpec as P

HEAD = 128
ROWS = 16
SLACK = 2
FAR = 2
HIDDEN_BY = 6
EARLY = 8
EARLY_BY = 18
DP = ("dp_0", "dp_1", "dp_2", "dp_3")
IN_VMEM = pl.BlockSpec(memory_space=pltpu.VMEM)
IN_SMEM = pl.BlockSpec(memory_space=pltpu.SMEM)
ANYWHERE = pl.BlockSpec(memory_space=pl.ANY)
BF16, F32 = jnp.bfloat16, jnp.float32


def copy_for_each(array, axis):
    count = lax.axis_size(axis)
    return lax.all_to_all(
        jnp.broadcast_to(array[None], (count, *array.shape)), axis, 0, 0, tiled=True
    )


def kernel_call(kernel, name, out_shape, specs, operands, scratch=(), out_spec=IN_VMEM, room=8):
    return pl.pallas_call(
        kernel,
        out_shape=out_shape,
        in_specs=specs,
        out_specs=jax.tree.map(lambda _: out_spec, out_shape),
        scratch_shapes=list(scratch),
        compiler_params=pltpu.CompilerParams(vmem_limit_bytes=room * 2**20),
        name=name,
    )(*operands)


def held_until(value, token):
    return pl.pallas_call(
        lambda value_ref, token_ref, out_ref: None,
        out_shape=jax.ShapeDtypeStruct(value.shape, value.dtype),
        in_specs=[ANYWHERE, ANYWHERE],
        out_specs=ANYWHERE,
        input_output_aliases={0: 0},
        compiler_params=pltpu.CompilerParams(vmem_limit_bytes=2**20),
        name="held_until",
    )(value, token)


def norm_kernel(where, x_ref, g_ref, *refs):
    *tiles, hidden_ref = refs
    _, tok, width = x_ref.shape
    across = len(tiles)
    near = width // (across * FAR)

    def one(index, carry):
        rows = pl.ds(pl.multiple_of(index * ROWS, ROWS), ROWS)
        for loop in range(2):
            x = x_ref[loop, rows, :].astype(F32)
            rinv = lax.rsqrt(jnp.mean(x * x, axis=-1, keepdims=True) + 1e-05)
            hidden_ref[...] = (x * rinv * g_ref[loop]).astype(BF16)
            for shift, tile_ref in enumerate(tiles):
                place = lax.rem(where[1] + shift, across)
                for half in range(FAR):
                    at = pl.multiple_of((half * across + place) * near, near)
                    tile_ref[loop, rows, half * near : (half + 1) * near] = hidden_ref[
                        :, pl.ds(at, near)
                    ]
        return carry

    lax.fori_loop(0, tok // ROWS, one, 0)


def rows_kernel(where, *refs):
    *sets, w_ref = refs
    wide, piece = sets[0].shape[1], sets[0].shape[0] // 32
    for index, ref in enumerate(sets):
        half, other = index % 2, index // 2
        core = (1 - where[2]) if other else where[2]

        def one(order, carry, half=half, core=core, ref=ref):
            outer, inner, depth = order // 8, order // 2 % 4, order % 2
            over_x, over_y = (inner, outer) if half == 0 else (outer, inner)
            z = lax.rem(where[3] + depth, 2)
            x = lax.rem(where[1] + 4 - over_x, 4)
            y = lax.rem(where[4] + 4 - over_y, 4)
            at = pl.multiple_of((((z * 4 + x) * 4 + y) * 2 + core) * piece, piece)
            came = pl.ds(pl.multiple_of(order * piece, piece), piece)
            w_ref[pl.ds(at, piece), half * wide : (half + 1) * wide] = ref[came, :]
            return carry

        lax.fori_loop(0, 32, one, 0)


def part_kernel(start, across, where, *refs):
    total = refs[2 * across][...] if start else None
    for tiles_ref, dv_ref in zip(refs[:across], refs[across : 2 * across], strict=True):
        tok = tiles_ref.shape[1]
        done = 0
        while done < dv_ref.shape[0]:
            loop, row = 1 - (start + done) // tok, (start + done) % tok
            count = min(tok - row, dv_ref.shape[0] - done)
            term = lax.dot_general(
                tiles_ref[loop, row : row + count, :],
                dv_ref[done : done + count, :],
                (((0,), (0,)), ((), ())),
                preferred_element_type=F32,
            )
            total = term if total is None else total + term
            done += count
    if not start:
        refs[-1][...] = total
        return
    keep_ref, give_ref, total_ref = refs[-3:]
    total_ref[...] = total
    count, piece, _ = keep_ref.shape
    for index in range(count):
        at = pl.multiple_of((2 * index + where[2]) * piece, piece)
        keep_ref[index] = total_ref[pl.ds(at, piece), :]
        at = pl.multiple_of((2 * index + 1 - where[2]) * piece, piece)
        give_ref[index] = total_ref[pl.ds(at, piece), :].astype(BF16)


def pair_kernel(keep_ref, got_ref, out_ref):
    out_ref[...] = (keep_ref[...] + got_ref[...].astype(F32)).astype(BF16)


def sum_kernel(pieces_ref, out_ref):
    total = pieces_ref[0].astype(F32)
    for index in range(1, pieces_ref.shape[0]):
        total = total + pieces_ref[index].astype(F32)
    out_ref[...] = total


def task_of(step, section, npipe):
    return step - SLACK * (npipe - 1 - section)


def step_kernel(step, npipe, blocks, where, w_ref, x_ref, g_ref, fresh_ref, in_ref, *refs):
    dx_ref, dv_ref = refs[-2:]
    section = where[0]
    task = task_of(step, section, npipe)

    @pl.when((task >= 0) & (task < 2 * blocks))
    def _():
        later = task < blocks
        loop = jnp.where(later, 1, 0)
        block = jnp.where(later, task, task - blocks)
        row = pl.multiple_of(block * ROWS, ROWS)
        width = dx_ref.shape[1]
        kv_width = dv_ref.shape[1]
        heads = kv_width // HEAD
        group = width // kv_width
        take = later & (section == npipe - 1)
        dy = jnp.where(take, fresh_ref[pl.ds(row, ROWS), :], in_ref[...]).astype(F32)
        x = x_ref[loop, pl.ds(row, ROWS), :].astype(F32)
        sums = []
        for head in range(heads):
            base = head * group * HEAD
            total = dy[:, base : base + HEAD]
            for member in range(1, group):
                at = base + member * HEAD
                total = total + dy[:, at : at + HEAD]
            sums.append(total)
        dv = jnp.concatenate(sums, axis=1).astype(BF16)
        dv_ref[...] = dv
        dh = lax.dot_general(
            dv, w_ref[...], (((1,), (1,)), ((), ())), preferred_element_type=F32
        )
        dhg = dh * g_ref[loop]
        rinv = lax.rsqrt(jnp.mean(x * x, axis=-1, keepdims=True) + 1e-05)
        normed = x * rinv
        along = jnp.mean(dhg * normed, axis=-1, keepdims=True)
        dx_ref[...] = (dy + rinv * (dhg - normed * along)).astype(BF16)


def collect_kernel(npipe, blocks, where, *refs):
    *pieces, out_ref, sems = refs
    section = where[0]

    def each(act):
        for step, piece in enumerate(pieces):
            task = task_of(step, section, npipe)

            @pl.when((task >= 0) & (task < 2 * blocks))
            def _():
                later = task < blocks
                loop = jnp.where(later, 1, 0)
                row = pl.multiple_of((task - jnp.where(later, 0, blocks)) * ROWS, ROWS)
                target = out_ref.at[loop, pl.ds(row, ROWS), :]
                act(pltpu.make_async_copy(piece, target, sems.at[step]))

    each(lambda copy: copy.start())
    each(lambda copy: copy.wait())


def stack_kernel(npipe, start, where, *refs):
    *pieces, out_ref = refs
    section = where[0]
    count = out_ref.shape[0] // ROWS
    for step, piece in enumerate(pieces):
        place = task_of(step, section, npipe) - start

        @pl.when((place >= 0) & (place < count))
        def _():
            out_ref[pl.ds(pl.multiple_of(place * ROWS, ROWS), ROWS), :] = piece[...]


def exchanged(pieces, axis):
    count = lax.axis_size(axis)
    moved = [pieces[0]]
    for shift in range(1, count):
        pairs = [(source, (source + shift) % count) for source in range(count)]
        moved.append(lax.ppermute(pieces[shift], axis, pairs))
    return moved


def on_device(saved, grad_out, gain, w_value):
    npipe = lax.axis_size("pipe")
    where = jnp.stack([lax.axis_index(name) for name in ("pipe", "dp_1", "dp_3", "dp_0", "dp_2")]).astype(jnp.int32)
    stage = lax.axis_index("pipe").astype(jnp.int32).reshape(1)
    x = saved[:, 0]
    _, tok, width = x.shape
    kv_width = w_value.shape[2]
    blocks = tok // ROWS
    across = lax.axis_size("dp_1")
    shape = jax.ShapeDtypeStruct

    tiles = kernel_call(
        norm_kernel,
        "normalize",
        (shape((2, tok, width // across), BF16),) * across,
        [IN_SMEM] + [IN_VMEM] * 2,
        (where, x, gain),
        scratch=(pltpu.VMEM((ROWS, width), BF16),),
    )
    own = w_value[0]
    pair = jnp.concatenate([own, lax.ppermute(own, DP[0], [(0, 1), (1, 0)])], axis=0)
    middle = kv_width // 2
    sets = []
    for part, axes in ((pair[:, :middle], ("dp_1", "dp_2")), (pair[:, middle:], ("dp_2", "dp_1"))):
        for axis in axes:
            if axis == axes[1] and not sets:
                part = held_until(part, tiles[0])
            part = jnp.concatenate(exchanged([part] * across, axis), axis=0)
        sets.append(part)
    sets += [lax.ppermute(part, DP[3], [(0, 1), (1, 0)]) for part in sets]
    hidden = exchanged(tiles, "dp_1")
    w_mat = kernel_call(
        rows_kernel,
        "rows",
        shape((width, kv_width), BF16),
        [IN_SMEM] + [IN_VMEM] * 4,
        (where, *sets),
    )

    def partial_sum(start, end, extra):
        rows, whole = (end - start) * ROWS, width // across
        dv = kernel_call(
            functools.partial(stack_kernel, npipe, start),
            "stack",
            shape((rows, kv_width), BF16),
            [IN_SMEM] + [IN_VMEM] * len(gv_parts),
            (stage, *gv_parts),
        )
        spread = exchanged([dv] * across, "dp_1")
        kinds = (shape(halves, F32), shape(halves, BF16)) if start else shape((whole, kv_width), F32)
        return kernel_call(
            functools.partial(part_kernel, start * ROWS, across),
            "part",
            kinds,
            [IN_SMEM] + [IN_VMEM] * (2 * across + len(extra)),
            (where, *hidden, *spread, *extra),
            scratch=(pltpu.VMEM((whole, kv_width), F32),) if start else (),
        )

    others = ("dp_0", "dp_2")
    count = lax.axis_size(others)
    halves = (count, w_value.shape[1], kv_width)
    steps = 2 * blocks + SLACK * (npipe - 1)
    sent, gx_parts, gv_parts = {}, [], []
    for step in range(steps):
        incoming = sent.pop(step - SLACK, None)
        if incoming is None:
            incoming = jnp.zeros((ROWS, width), BF16)
        later = ()
        if step == HIDDEN_BY:
            later = tuple(hidden[1:])
        elif step == EARLY_BY:
            later = (early,)
        turn = gv_parts[-1:]
        dx, dv = kernel_call(
            functools.partial(step_kernel, step, npipe, blocks),
            "section_step",
            (shape((ROWS, width), BF16), shape((ROWS, kv_width), BF16)),
            [IN_SMEM] + [IN_VMEM] * (5 + len(turn)) + [ANYWHERE] * len(later),
            (stage, w_mat, x, gain, grad_out, incoming, *turn, *later),
        )
        gx_parts.append(dx)
        gv_parts.append(dv)
        pairs = []
        for source in range(npipe):
            task = task_of(step, source, npipe)
            if 0 <= task < (blocks if source == 0 else 2 * blocks):
                pairs.append((source, (source - 1) % npipe))
        if pairs:
            sent[step] = lax.ppermute(dx, "pipe", pairs)
        if step == EARLY + SLACK * (npipe - 1) - 1:
            early = partial_sum(0, EARLY, ())

    grad_x = kernel_call(
        functools.partial(collect_kernel, npipe, blocks),
        "collect_rows",
        shape((2, tok, width), BF16),
        [IN_SMEM] + [IN_VMEM] * steps,
        (stage, *gx_parts),
        scratch=(pltpu.SemaphoreType.DMA((steps,)),),
        out_spec=ANYWHERE,
    )[:, None]
    keep, give = partial_sum(EARLY, 2 * blocks, (early,))
    got = lax.ppermute(give, DP[3], [(0, 1), (1, 0)])
    paired = kernel_call(pair_kernel, "pair", shape(halves, BF16), [IN_VMEM] * 2, (keep, got))
    landed = lax.all_to_all(paired, others, 0, 0, tiled=True)
    grad_w = kernel_call(sum_kernel, "sum", shape(halves[1:], F32), [IN_VMEM], (landed,))[None]
    return (grad_x, grad_w)


def solution(mesh):
    finer = Mesh(
        mesh.devices.reshape(mesh.shape["pipe"], 2, 4, 4, 2),
        ("pipe", "dp_0", "dp_1", "dp_2", "dp_3"),
    )
    placed = (P(None, "pipe", DP, None), P(DP, None), P(None, "pipe", None), P("pipe", DP, None))
    return jax.shard_map(
        on_device,
        mesh=finer,
        in_specs=placed,
        out_specs=(P(None, "pipe", DP, None), P("pipe", DP, None)),
        check_vma=False,
    )
```
